32 devices in a mesh: sector: 16 (over z, y, x), term: 2 (over core).
Axes of the slice: x: 2, y: 2, z: 4, core: 2. Of those that a mesh axis runs over, the one named last changes fastest.
Arguments:
- psi: bfloat16 [4, 16, 4, 256, 256], P(None, 'sector'), may hold values from -6 to 6
- left_env: bfloat16 [4, 16, 256, 256], P('term', 'sector'), may hold values from -0.375 to 0.375
- right_env: bfloat16 [4, 16, 256, 256], P('term', 'sector'), may hold values from -0.375 to 0.375
- op_index: int32 [4], P('term'), may hold values from 0 to 4
- kept_rows: int32 [16], P('sector'), may hold values from 64 to 256, as said below
Outputs:
- sigma: float32 [4, 16, 4, 256, 256], P(None, 'sector', None, 'term')
The draws below stay inside these ranges and needn't reach their ends.
Inputs may be any that keep to these rules, and one draw needn't show every extreme that they name: `kept_rows`: some sector keeps all 256 rows and some other keeps 256 // 4.
All inputs are finite; a program needn't handle non-finite values.
Results may differ from the reference program's by a relative error of at most 0.0029.
Values may be sent and summed in bfloat16 or wider, within the bound.
No kernel may reach another device: no remote copies, remote signals or barrier semaphores. Data moves between devices by JAX's collectives and lax.ppermute only.
A program may use at most 64 MiB of HBM per device.

```python
import jax
import jax.numpy as jnp
from jax import lax

B = 256
PHYS = 4
OP_KINDS = 5
NVEC = 4
TERMS = 4
SECTORS = 16


def draw_kept_rows(key, part):
    key_sizes, key_full, key_small = jax.random.split(jax.random.fold_in(key, 17), 3)
    counts = jax.random.randint(key_sizes, (SECTORS,), B // 4, B + 1, dtype=jnp.int32)
    full_index = jax.random.randint(key_full, (), 0, SECTORS, dtype=jnp.int32)
    small_index = (full_index + 1 + jax.random.randint(key_small, (), 0, SECTORS - 1, dtype=jnp.int32)) % SECTORS
    counts = counts.at[full_index].set(B).at[small_index].set(B // 4)
    return counts


def place_ends(drawn, stream_key, smallest, top_value):
    spot = [jax.random.randint(jax.random.fold_in(stream_key, axis), (), 0, length) for axis, length in enumerate(drawn.shape)]
    widest = drawn.shape.index(max(drawn.shape))
    neighbour = spot[:widest] + [(spot[widest] + 1) % drawn.shape[widest]] + spot[widest + 1:]
    return drawn.at[tuple(spot)].set(smallest).at[tuple(neighbour)].set(top_value)


def level_of(stream_key, shape, pieces, smallest, top_value):
    gain, own = 1.0, jax.random.fold_in(stream_key, 6)
    for position, parts in pieces:
        steps = jnp.exp(jax.random.uniform(jax.random.fold_in(own, position), (parts,), jnp.float32, smallest / len(pieces), top_value / len(pieces)))
        gain = gain * jnp.repeat(steps, shape[position] // parts).reshape([-1 if axis == position else 1 for axis in range(len(shape))])
    return gain


def normal_values(key, extent, scale, reach, shards=(), held_as=jnp.bfloat16):
    entries = jax.random.normal(key, extent, jnp.float32) * scale
    if len(shards) > 0:
        entries = level_of(key, extent, shards, -0.22, 0.18) * entries
    return jnp.clip(entries, min=-reach, max=reach).astype(held_as)


def setup_inputs(seed: int = 0) -> dict:
    keys = jax.random.split(jax.random.key(seed), 6)
    psi = normal_values(keys[0], (NVEC, SECTORS, PHYS, B, B), 1.0, 6.0, ((1, 16),))
    left_env = normal_values(keys[1], (TERMS, SECTORS, B, B), B ** -0.5, 0.375, ((0, 2), (1, 16)))
    right_env = normal_values(keys[2], (TERMS, SECTORS, B, B), B ** -0.5, 0.375, ((0, 2), (1, 16)))
    op_index = place_ends(jax.random.randint(keys[3], (TERMS,), 0, OP_KINDS), jax.random.fold_in(keys[3], 1), 0, OP_KINDS - 1).astype(jnp.int32)
    kept_rows = draw_kept_rows(jax.random.fold_in(keys[5], 71), 0)
    return {"psi": psi, "left_env": left_env, "right_env": right_env, "op_index": op_index, "kept_rows": kept_rows}


def diagonal_matrix(values):
    return [[values[r] if r == c else 0.0 for c in range(4)] for r in range(4)]


def operator_table():
    flip = [[0.0, 0.0, 0.0, 0.0], [0.0, 0.0, 0.5, 0.0], [0.0, 0.5, 0.0, 0.0], [0.0, 0.0, 0.0, 0.0]]
    stacked = [diagonal_matrix([1.0, 1.0, 1.0, 1.0]), diagonal_matrix([0.25, -0.25, -0.25, 0.25]), flip, diagonal_matrix([0.5, 0.5, -0.5, -0.5]), diagonal_matrix([0.5, -0.5, 0.5, -0.5])]
    return jnp.asarray(stacked, jnp.float32)


def reference(psi, left_env, right_env, op_index, kept_rows):
    onehot = (op_index[:, None] == jnp.arange(OP_KINDS, dtype=jnp.int32)[None, :]).astype(jnp.float32)
    term_factor = jnp.einsum("tk,kpq->tpq", onehot, operator_table(), precision=lax.Precision.HIGHEST)
    trial_vectors = psi.astype(jnp.float32)
    zeros_block = jnp.zeros((1, B, B), jnp.float32)

    def per_term(running, inputs_per_term):
        left_mat, right_mat, coeff_mat = inputs_per_term
        lifted = jnp.einsum("sab,vspbc->vspac", left_mat.astype(jnp.float32), trial_vectors, precision=lax.Precision.HIGHEST)
        lifted = lax.optimization_barrier(lifted.astype(jnp.bfloat16)).astype(jnp.float32)
        right_f = right_mat.astype(jnp.float32)
        upper_right_block = jnp.concatenate([right_f[1:], zeros_block], 0)
        right_down = jnp.concatenate([zeros_block, right_f[:-1]], 0)
        chosen = jnp.stack([upper_right_block, right_f, right_f, right_down], 1)
        mapped_vectors = jnp.einsum("vspac,spdc->vspad", lifted, chosen, precision=lax.Precision.HIGHEST)
        running = running + jnp.einsum("pq,vsqad->vspad", coeff_mat, mapped_vectors, precision=lax.Precision.HIGHEST)
        return running, None

    start = jnp.zeros((NVEC, SECTORS, PHYS, B, B), jnp.float32)
    summed, _ = lax.scan(per_term, start, (left_env, right_env, term_factor))
    zero_count = jnp.zeros((1,), jnp.int32)
    kept_up = jnp.concatenate([kept_rows[1:], zero_count], 0)
    kept_down = jnp.concatenate([zero_count, kept_rows[:-1]], 0)
    column_kept = jnp.stack([kept_up, kept_rows, kept_rows, kept_down], 1)
    row_ids = jnp.arange(B, dtype=jnp.int32)
    keep_mask = (row_ids[None, None, :, None] < kept_rows[:, None, None, None]) & (row_ids[None, None, None, :] < column_kept[:, :, None, None])
    return jnp.where(keep_mask[None], summed, 0.0)
```

```python
import jax
import jax.numpy as jnp
from jax import lax
from jax.experimental import pallas as pl
from jax.experimental.pallas import tpu as pltpu
from jax.sharding import PartitionSpec as P

FLIP = 2
COEFFICIENTS = (
    (1.0, 1.0, 1.0, 1.0),
    (0.25, -0.25, -0.25, 0.25),
    (0.0, 0.5, 0.5, 0.0),
    (0.5, 0.5, -0.5, -0.5),
    (0.5, -0.5, 0.5, -0.5),
)
EXTRA = 16
VMEM_LIMIT = 40 * 1024 * 1024
VMEM = pl.BlockSpec(memory_space=pltpu.VMEM)
SMEM = pl.BlockSpec(memory_space=pltpu.SMEM)
ANY = pl.BlockSpec(memory_space=pl.ANY)


def coefficient(op, p):
    value = jnp.float32(COEFFICIENTS[-1][p])
    for kind in range(len(COEFFICIENTS) - 1):
        value = jnp.where(op == kind, jnp.float32(COEFFICIENTS[kind][p]), value)
    return value


def times_transpose(a, b):
    return lax.dot_general(a, b, (((1,), (1,)), ((), ())), preferred_element_type=jnp.float32)


def centre_kernel(pos, kept, op_own, op_other, psi, left_own, left_other, right_own, right_other,
                  sigma, rim, psi_buf, lefts, centre, out_buf, psi_sem, out_sem):
    nvec = psi.shape[0]
    own, half, size = left_own.shape[0], sigma.shape[3], psi.shape[4]
    terms = own + left_other.shape[0]
    loads = [pltpu.make_async_copy(psi.at[v, 0], psi_buf.at[v], psi_sem.at[v]) for v in range(nvec)]
    for load in loads:
        load.start()
    first_row, state_a = pl.multiple_of(pos[0], half), pos[1]
    for t in range(terms):
        source, k = (left_own, t) if t < own else (left_other, t - own)
        lefts[pl.ds(t * half, half), :] = source[k, 0, pl.ds(first_row, half), :]
    ops = [op_own[t] if t < own else op_other[t - own] for t in range(terms)]
    for v in range(nvec):
        loads[v].wait()
        for q in range(4):
            lifted = jnp.dot(lefts[...], psi_buf[v, q], preferred_element_type=jnp.float32)
            for t in range(terms):
                part = lifted[t * half:(t + 1) * half]
                if q in (0, 3):
                    block = (part * coefficient(ops[t], q)).astype(jnp.bfloat16)
                    slot = jnp.where(state_a == q, 0, 1)
                    rim[slot, t, pl.ds(v * half, half), :] = block
                else:
                    flipped = ops[t] == FLIP
                    factor = jnp.where(flipped, coefficient(ops[t], 3 - q), coefficient(ops[t], q))
                    slot = jnp.where(flipped, 2 - q, q - 1)
                    centre[t, pl.ds((slot * nvec + v) * half, half), :] = (part * factor).astype(
                        jnp.bfloat16
                    )
    rows = lax.broadcasted_iota(jnp.int32, (half, size), 0) + first_row
    cols = lax.broadcasted_iota(jnp.int32, (half, size), 1)
    keep = (rows < kept[0]) & (cols < kept[0])
    for slot in range(2):
        total = None
        for t in range(terms):
            r = right_own[t, 0] if t < own else right_other[t - own, 0]
            part = times_transpose(centre[t, pl.ds(slot * nvec * half, nvec * half), :], r)
            total = part if total is None else total + part
        for v in range(nvec):
            out_buf[slot, v] = jnp.where(keep, total[v * half:(v + 1) * half], 0.0)
        pltpu.make_async_copy(out_buf.at[slot], sigma.at[:, 0, slot + 1], out_sem.at[slot]).start()
    for slot in range(2):
        pltpu.make_async_copy(out_buf.at[slot], sigma.at[:, 0, slot + 1], out_sem.at[slot]).wait()


def make_rim_kernel(which):
    def kernel(pos, kept, rim, right_own, right_other, sigma_in, sigma, out_buf, out_sem):
        nvec, half, size = out_buf.shape
        terms = rim.shape[1]
        own = terms // 2 if right_own.shape[0] != right_other.shape[0] else 0
        total = None
        for t in range(terms):
            source, k = (right_own, t) if t < own else (right_other, t - own)
            part = times_transpose(rim[which, t], source[k * size:(k + 1) * size])
            total = part if total is None else total + part
        note = right_own if right_own.shape[0] > right_other.shape[0] else right_other
        edge = note[own * size:own * size + 1].astype(jnp.float32)
        rows = lax.broadcasted_iota(jnp.int32, (half, size), 0) + pos[0]
        cols = lax.broadcasted_iota(jnp.int32, (half, size), 1).astype(jnp.float32)
        keep = (rows < kept[0]) & (cols < edge) & (pos[3 + which] > 0)
        for v in range(nvec):
            out_buf[v] = jnp.where(keep, total[v * half:(v + 1) * half], 0.0)
        copy = pltpu.make_async_copy(out_buf, sigma.at[:, 0, pos[1 + which]], out_sem)
        copy.start()
        copy.wait()

    return kernel


def with_note(blocks, kept_rows):
    size = blocks.shape[-1]
    note = jnp.broadcast_to(kept_rows.astype(blocks.dtype)[:, None], (EXTRA, size))
    return jnp.concatenate([blocks.reshape(-1, size), note], 0)


def two_core_cycle(sectors):
    up = [(2 * i, 2 * i + 2) for i in range(sectors - 1)]
    down = [(2 * i + 3, 2 * i + 1) for i in range(sectors - 1)]
    return up + [(2 * sectors - 2, 2 * sectors - 1)] + down + [(1, 0)]


def shards(psi, left_env, right_env, op_index, kept_rows):
    sectors, cores = lax.axis_size("sector"), lax.axis_size("term")
    me, core = lax.axis_index("sector"), lax.axis_index("term")
    nvec, size = psi.shape[0], psi.shape[-1]
    half = size // cores
    terms = left_env.shape[0] * cores
    has_below, has_above = me > 0, me < sectors - 1
    swap = [(0, 1), (1, 0)]

    if cores == 2:
        below_is_a = core == 0
        cycle = two_core_cycle(sectors)
        reverse = [(b, a) for a, b in cycle]
        own_a = lax.ppermute(right_env, ("sector", "term"), cycle)
        own_b = lax.ppermute(with_note(right_env, kept_rows), ("sector", "term"), reverse)
        left_own, right_own, op_own = left_env, right_env, op_index
        left_other = lax.ppermute(left_env, "term", swap)
        right_other = lax.ppermute(right_env, "term", swap)
        op_other = lax.ppermute(op_index, "term", swap)
    else:
        below_is_a = core >= 0
        forward = [(i, i + 1) for i in range(sectors - 1)]
        backward = [(b, a) for a, b in forward]
        gathered = [lax.all_gather(x, "term", tiled=True) for x in (left_env, right_env, op_index)]
        (left_own, left_other), (right_own, right_other), (op_own, op_other) = [
            jnp.split(x, 2) for x in gathered
        ]

        def neighbour(pairs):
            blocks = lax.all_gather(lax.ppermute(right_env, "sector", pairs), "term", tiled=True)
            first, second = jnp.split(blocks, 2)
            return first, second, lax.ppermute(kept_rows, "sector", pairs)

        own_a, other_a, kept_a = neighbour(forward)
        own_b, other_b, kept_b = neighbour(backward)
        other_a, own_b = with_note(other_a, kept_a), with_note(own_b, kept_b)

    state_a = jnp.where(below_is_a, 3, 0)
    has_a = jnp.where(below_is_a, has_below, has_above)
    has_b = jnp.where(below_is_a, has_above, has_below)
    pos = jnp.stack([core * half, state_a, 3 - state_a, has_a, has_b]).astype(jnp.int32)

    sigma_shape = jax.ShapeDtypeStruct((nvec, 1, 4, half, size), jnp.float32)
    rim_shape = jax.ShapeDtypeStruct((2, terms, nvec * half, size), jnp.bfloat16)
    block = size * size
    sigma, rim = pl.pallas_call(
        centre_kernel,
        out_shape=(sigma_shape, rim_shape),
        in_specs=[SMEM, SMEM, SMEM, SMEM, ANY, VMEM, VMEM, VMEM, VMEM],
        out_specs=(ANY, VMEM),
        scratch_shapes=[
            pltpu.VMEM((nvec, 4, size, size), jnp.bfloat16),
            pltpu.VMEM((terms * half, size), jnp.bfloat16),
            pltpu.VMEM((terms, 2 * nvec * half, size), jnp.bfloat16),
            pltpu.VMEM((2, nvec, half, size), jnp.float32),
            pltpu.SemaphoreType.DMA((nvec,)),
            pltpu.SemaphoreType.DMA((2,)),
        ],
        compiler_params=pltpu.CompilerParams(vmem_limit_bytes=VMEM_LIMIT),
        cost_estimate=pl.CostEstimate(
            flops=12 * nvec * terms * half * block, bytes_accessed=14 * nvec * block, transcendentals=0
        ),
        name="centre",
    )(pos, kept_rows, op_own, op_other, psi, left_own, left_other, right_own, right_other)

    def finish(which, sigma, rim, right_own, right_other):
        return pl.pallas_call(
            make_rim_kernel(which),
            out_shape=sigma_shape,
            in_specs=[SMEM, SMEM, VMEM, VMEM, VMEM, ANY],
            out_specs=ANY,
            scratch_shapes=[pltpu.VMEM((nvec, half, size), jnp.float32), pltpu.SemaphoreType.DMA],
            input_output_aliases={5: 0},
            compiler_params=pltpu.CompilerParams(vmem_limit_bytes=VMEM_LIMIT),
            cost_estimate=pl.CostEstimate(
                flops=2 * nvec * terms * half * block, bytes_accessed=4 * nvec * block, transcendentals=0
            ),
            name="rim",
        )(pos, kept_rows, rim, right_own, right_other, sigma)

    own_a, sigma, rim = lax.optimization_barrier((own_a.reshape(-1, size), sigma, rim))
    if cores == 2:
        other_b = lax.ppermute(own_a, "term", swap)
        own_b, other_b = lax.optimization_barrier((own_b, other_b))
        other_a = lax.ppermute(own_b, "term", swap)
    sigma = finish(1, sigma, rim, own_b, other_b.reshape(-1, size))
    return finish(0, sigma, rim, own_a, other_a)


def solution(mesh):
    in_specs = (
        P(None, "sector", None, None, None),
        P("term", "sector", None, None),
        P("term", "sector", None, None),
        P("term"),
        P("sector"),
    )
    out_specs = P(None, "sector", None, "term", None)
    return jax.shard_map(shards, mesh=mesh, in_specs=in_specs, out_specs=out_specs, check_vma=False)
```

```python
import jax
import jax.numpy as jnp
from jax import lax
from jax.experimental import pallas as pl
from jax.experimental.pallas import tpu as pltpu
from jax.sharding import PartitionSpec as P

FLIP = 2
COEFFICIENTS = (
    (1.0, 1.0, 1.0, 1.0),
    (0.25, -0.25, -0.25, 0.25),
    (0.0, 0.5, 0.5, 0.0),
    (0.5, 0.5, -0.5, -0.5),
    (0.5, -0.5, 0.5, -0.5),
)
VMEM_LIMIT = 16 * 1024 * 1024
CENTRE_LIMIT = 50 * 1024 * 1024
VMEM = pl.BlockSpec(memory_space=pltpu.VMEM)
SMEM = pl.BlockSpec(memory_space=pltpu.SMEM)
HBM = pl.BlockSpec(memory_space=pltpu.HBM)


def coefficient(op, p):
    value = jnp.float32(COEFFICIENTS[-1][p])
    for kind in range(len(COEFFICIENTS) - 1):
        value = jnp.where(op == kind, jnp.float32(COEFFICIENTS[kind][p]), value)
    return value


def times_transpose(a, b):
    return lax.dot_general(a, b, (((1,), (1,)), ((), ())), preferred_element_type=jnp.float32)


def below_is_a():
    return lax.axis_index("term") == 0 if lax.axis_size("term") == 2 else True


def centre_kernel(pos, psi, left_own, left_other, right_own, right_other, sigma, rim, kept_row,
                  psi_buf, left_buf, right_buf, lefts, centre, out_buf, psi_sem, env_sem, out_sem):
    nvec = psi.shape[0]
    own, half, size = left_own.shape[0], sigma.shape[3], psi.shape[4]
    terms = own + left_other.shape[0]
    envs = [
        pltpu.make_async_copy(left_own.at[:, 0], left_buf, env_sem.at[0]),
        pltpu.make_async_copy(right_own.at[:, 0], right_buf, env_sem.at[1]),
    ]
    loads = [pltpu.make_async_copy(psi.at[v, 0], psi_buf.at[v], psi_sem.at[v]) for v in range(nvec)]
    for copy in [envs[0]] + loads + [envs[1]]:
        copy.start()
    first_row = pl.multiple_of(lax.axis_index("term") * half, half)
    slot_of_3 = jnp.where(below_is_a(), 0, 1)
    kept = pos[0]
    ops = [pos[1 + t] for t in range(terms)]
    kept_row[...] = jnp.full(kept_row.shape, kept, jnp.float32)
    envs[0].wait()
    for t in range(own):
        lefts[pl.ds(t * half, half), :] = left_buf[t, pl.ds(first_row, half), :]
    for t in range(own, terms):
        lefts[pl.ds(t * half, half), :] = left_other[t - own, 0, pl.ds(first_row, half), :]
    for v in range(nvec):
        loads[v].wait()
        for q in range(4):
            lifted = jnp.dot(lefts[...], psi_buf[v, q], preferred_element_type=jnp.float32)
            for t in range(terms):
                part = lifted[t * half:(t + 1) * half]
                if q in (0, 3):
                    slot = slot_of_3 if q == 3 else 1 - slot_of_3
                    block = (part * coefficient(ops[t], q)).astype(jnp.bfloat16)
                    rim[slot, t, pl.ds(v * half, half), :] = block
                else:
                    flipped = ops[t] == FLIP
                    factor = jnp.where(flipped, coefficient(ops[t], 3 - q), coefficient(ops[t], q))
                    slot = jnp.where(flipped, 2 - q, q - 1)
                    block = (part * factor).astype(jnp.bfloat16)
                    centre[t, pl.ds((slot * nvec + v) * half, half), :] = block
    rows = lax.broadcasted_iota(jnp.int32, (half, size), 0) + first_row
    keep = (rows < kept) & (lax.broadcasted_iota(jnp.int32, (half, size), 1) < kept)
    envs[1].wait()
    stores = []
    for slot in range(2):
        total = None
        for t in range(terms):
            right = right_buf[t] if t < own else right_other[t - own, 0]
            part = times_transpose(centre[t, pl.ds(slot * nvec * half, nvec * half), :], right)
            total = part if total is None else total + part
        for v in range(nvec):
            out_buf[slot, v] = jnp.where(keep, total[v * half:(v + 1) * half], 0.0)
        stores.append(
            pltpu.make_async_copy(out_buf.at[slot], sigma.at[:, 0, slot + 1], out_sem.at[slot])
        )
        stores[-1].start()
    for store in stores:
        store.wait()


def sum_terms(rim, which, first, blocks, count, rows, total=None):
    size = rim.shape[-1]
    for k in range(count):
        product = times_transpose(rim[which, first + k, rows, :], blocks[k * size:(k + 1) * size])
        total = product if total is None else total + product
    return total


def state_mask(which, kept_row, note, half):
    is_below = (which == 0) == below_is_a()
    me = lax.axis_index("sector")
    there = jnp.where(is_below, me, lax.axis_size("sector") - 1 - me) > 0
    shape = (half, kept_row.shape[1])
    rows = lax.broadcasted_iota(jnp.int32, shape, 0) + lax.axis_index("term") * half
    cols = lax.broadcasted_iota(jnp.int32, shape, 1)
    keep = (rows.astype(jnp.float32) < kept_row[0:1, :]) & there
    return keep & (cols.astype(jnp.float32) < note[0:1, :]), jnp.where(is_below, 3, 0)


def own_rim_kernel(rim, own_a, own_b, part_a, part_b):
    count, rows = own_a.shape[0] // rim.shape[-1], pl.ds(0, rim.shape[2])
    part_a[...] = sum_terms(rim, 0, 0, own_a, count, rows)
    part_b[...] = sum_terms(rim, 1, 0, own_b, count, rows)


def last_rim_kernel(kept_row, note_a, note_b, rim, other_a, other_b, part_a, part_b, sigma_in, sigma,
                    out_buf, out_sem):
    _, nvec, half, size = out_buf.shape
    count, groups = other_a.shape[0] // size, out_sem.shape[1]
    first, per_group = rim.shape[1] - count, nvec // groups
    stores = []
    for which, note, blocks, part in ((0, note_a, other_a, part_a), (1, note_b, other_b, part_b)):
        keep, state = state_mask(which, kept_row, note, half)
        for group in range(groups):
            rows = pl.ds(group * per_group * half, per_group * half)
            total = sum_terms(rim, which, first, blocks, count, rows, part[rows, :])
            for j in range(per_group):
                out_buf[which, group * per_group + j] = jnp.where(
                    keep, total[j * half:(j + 1) * half], 0.0
                )
            vectors = pl.ds(group * per_group, per_group)
            store = pltpu.make_async_copy(
                out_buf.at[which, vectors], sigma.at[vectors, 0, state], out_sem.at[which, group]
            )
            store.start()
            stores.append(store)
    for store in stores:
        store.wait()


def note_of(kept_rows, size):
    return jnp.broadcast_to(kept_rows.astype(jnp.float32)[:, None], (8, size))


def two_core_cycle(sectors):
    up = [(2 * i, 2 * i + 2) for i in range(sectors - 1)]
    down = [(2 * i + 3, 2 * i + 1) for i in range(sectors - 1)]
    return up + [(2 * sectors - 2, 2 * sectors - 1)] + down + [(1, 0)]


def shards(psi, left_env, right_env, op_index, kept_rows):
    sectors, cores = lax.axis_size("sector"), lax.axis_size("term")
    nvec, size = psi.shape[0], psi.shape[-1]
    half = size // cores
    terms = left_env.shape[0] * cores
    swap = [(0, 1), (1, 0)]

    if cores == 2:
        cycle = two_core_cycle(sectors)
        reverse = [(b, a) for a, b in cycle]
        own_a = lax.ppermute(right_env, ("sector", "term"), cycle)
        own_b = lax.ppermute(right_env, ("sector", "term"), reverse)
        note_a = lax.ppermute(note_of(kept_rows, size), ("sector", "term"), cycle)
        left_own, right_own, op_own = left_env, right_env, op_index
        left_other = lax.ppermute(left_env, "term", swap)
        right_other = lax.ppermute(right_env, "term", swap)
        op_other = lax.ppermute(op_index, "term", swap)
    else:
        forward = [(i, i + 1) for i in range(sectors - 1)]
        backward = [(b, a) for a, b in forward]
        gathered = [lax.all_gather(x, "term", tiled=True) for x in (left_env, right_env, op_index)]
        (left_own, left_other), (right_own, right_other), (op_own, op_other) = [
            jnp.split(x, 2) for x in gathered
        ]

        def neighbour(pairs):
            blocks = lax.all_gather(lax.ppermute(right_env, "sector", pairs), "term", tiled=True)
            note = lax.ppermute(note_of(kept_rows, size), "sector", pairs)
            return *jnp.split(blocks, 2), note

        own_a, other_a, note_a = neighbour(forward)
        own_b, other_b, note_b = neighbour(backward)

    pos = jnp.concatenate([kept_rows, op_own, op_other])
    sigma_shape = jax.ShapeDtypeStruct((nvec, 1, 4, half, size), jnp.float32)
    rim_shape = jax.ShapeDtypeStruct((2, terms, nvec * half, size), jnp.bfloat16)
    part_shape = jax.ShapeDtypeStruct((nvec * half, size), jnp.float32)
    kept_shape = jax.ShapeDtypeStruct((8, size), jnp.float32)
    params = pltpu.CompilerParams(vmem_limit_bytes=VMEM_LIMIT)

    groups = 2 if nvec % 2 == 0 else 1
    sigma, rim, kept_row = pl.pallas_call(
        centre_kernel,
        out_shape=(sigma_shape, rim_shape, kept_shape),
        in_specs=[SMEM, HBM, HBM, VMEM, HBM, VMEM],
        out_specs=(HBM, VMEM, VMEM),
        scratch_shapes=[
            pltpu.VMEM((nvec, 4, size, size), jnp.bfloat16),
            pltpu.VMEM((left_own.shape[0], size, size), jnp.bfloat16),
            pltpu.VMEM((right_own.shape[0], size, size), jnp.bfloat16),
            pltpu.VMEM((terms * half, size), jnp.bfloat16),
            pltpu.VMEM((terms, 2 * nvec * half, size), jnp.bfloat16),
            pltpu.VMEM((2, nvec, half, size), jnp.float32),
            pltpu.SemaphoreType.DMA((nvec,)),
            pltpu.SemaphoreType.DMA((2,)),
            pltpu.SemaphoreType.DMA((2,)),
        ],
        compiler_params=pltpu.CompilerParams(vmem_limit_bytes=CENTRE_LIMIT),
        name="centre",
    )(pos, psi, left_own, left_other, right_own, right_other)

    own_a, own_b, note_a, sigma, rim = lax.optimization_barrier((own_a, own_b, note_a, sigma, rim))
    if cores == 2:
        other_b = lax.ppermute(own_a, "term", swap)
        other_a = lax.ppermute(own_b, "term", swap)
        note_b = lax.ppermute(note_a, "term", swap)
    own_a, own_b, other_a, other_b = [
        x.reshape(-1, size) for x in (own_a, own_b, other_a, other_b)
    ]
    part_a, part_b = pl.pallas_call(
        own_rim_kernel,
        out_shape=(part_shape, part_shape),
        in_specs=[VMEM] * 3,
        out_specs=(VMEM, VMEM),
        compiler_params=params,
        name="own_rim",
    )(rim, own_a, own_b)
    return pl.pallas_call(
        last_rim_kernel,
        out_shape=sigma_shape,
        in_specs=[VMEM] * 8 + [HBM],
        out_specs=HBM,
        scratch_shapes=[
            pltpu.VMEM((2, nvec, half, size), jnp.float32),
            pltpu.SemaphoreType.DMA((2, groups)),
        ],
        input_output_aliases={8: 0},
        compiler_params=params,
        name="last_rim",
    )(kept_row, note_a, note_b, rim, other_a, other_b, part_a, part_b, sigma)


def solution(mesh):
    in_specs = (
        P(None, "sector", None, None, None),
        P("term", "sector", None, None),
        P("term", "sector", None, None),
        P("term"),
        P("sector"),
    )
    out_specs = P(None, "sector", None, "term", None)
    return jax.shard_map(shards, mesh=mesh, in_specs=in_specs, out_specs=out_specs, check_vma=False)
```

```python
import jax
import jax.numpy as jnp
from jax import lax
from jax.experimental import pallas as pl
from jax.experimental.pallas import tpu as pltpu
from jax.sharding import PartitionSpec as P

FLIP = 2
COEFFICIENTS = (
    (1.0, 1.0, 1.0, 1.0),
    (0.25, -0.25, -0.25, 0.25),
    (0.0, 0.5, 0.5, 0.0),
    (0.5, 0.5, -0.5, -0.5),
    (0.5, -0.5, 0.5, -0.5),
)
VMEM_LIMIT = 16 * 1024 * 1024
CENTRE_LIMIT = 50 * 1024 * 1024
PACK_LIMIT = 54579 * 1024
VMEM = pl.BlockSpec(memory_space=pltpu.VMEM)
HBM = pl.BlockSpec(memory_space=pltpu.HBM)


def coefficient(op, p):
    value = jnp.full_like(op, COEFFICIENTS[-1][p])
    for kind in range(len(COEFFICIENTS) - 1):
        value = jnp.where(op == kind, COEFFICIENTS[kind][p], value)
    return value


def times_transpose(a, b):
    return lax.dot_general(a, b, (((1,), (1,)), ((), ())), preferred_element_type=jnp.float32)


def below_is_a():
    return lax.axis_index("term") == 0 if lax.axis_size("term") == 2 else True


def info_rows(terms):
    return 8 * pl.cdiv(1 + terms, 8)


def info_of(kept, ops, terms, size):
    rows = lax.broadcasted_iota(jnp.int32, (info_rows(terms), size), 0)
    info = jnp.where(rows == 0, kept[0], 0)
    for t in range(terms):
        info = jnp.where(rows == 1 + t, ops[t], info)
    return info.astype(jnp.float32)


def pack_kernel(kept, ops, left, right, info, mine, theirs, *refs):
    *blocks, kept_buf, ops_buf, sems = refs
    terms, half, size = mine.shape
    core = lax.axis_index("term")
    scalars = [
        pltpu.make_async_copy(kept, kept_buf, sems.at[0]),
        pltpu.make_async_copy(ops, ops_buf, sems.at[1]),
    ]
    copies = [
        pltpu.make_async_copy(
            left.at[:, 0, pl.ds(pl.multiple_of(who * half, half), half)], rows, sems.at[2 + k]
        )
        for k, (who, rows) in enumerate(((core, mine), (1 - core, theirs)))
    ]
    for t, block in enumerate(blocks):
        copies.append(pltpu.make_async_copy(right.at[t, 0], block, sems.at[4 + t]))
    for copy in scalars + copies:
        copy.start()
    for copy in scalars:
        copy.wait()
    info[...] = info_of(kept_buf, ops_buf, terms, size)
    for copy in copies:
        copy.wait()


def pack(kept, ops, left, right, half):
    terms, size = left.shape[0], left.shape[-1]
    rows = jax.ShapeDtypeStruct((terms, half, size), left.dtype)
    block = jax.ShapeDtypeStruct((size, size), right.dtype)
    info, mine, theirs, *blocks = pl.pallas_call(
        pack_kernel,
        out_shape=(jax.ShapeDtypeStruct((info_rows(terms), size), jnp.float32), rows, rows)
        + (block,) * terms,
        in_specs=[HBM] * 4,
        out_specs=(VMEM,) * (3 + terms),
        scratch_shapes=[
            pltpu.SMEM(kept.shape, kept.dtype),
            pltpu.SMEM(ops.shape, ops.dtype),
            pltpu.SemaphoreType.DMA((4 + terms,)),
        ],
        compiler_params=pltpu.CompilerParams(vmem_limit_bytes=PACK_LIMIT),
        name="pack",
    )(kept, ops, left, right)
    return info, mine, theirs, blocks


def centre_kernel(psi, info_own, info_other, left_own, left_other, *refs):
    (*rights, sigma, rim, psi_buf, lefts, centre, out_buf, psi_sem, out_sem) = refs
    nvec, half, size = psi.shape[0], sigma.shape[3], psi.shape[4]
    own, terms = left_own.shape[0], len(rights)
    loads = [pltpu.make_async_copy(psi.at[v, 0], psi_buf.at[v], psi_sem.at[v]) for v in range(nvec)]
    for copy in loads:
        copy.start()
    for t in range(terms):
        source, k = (left_own, t) if t < own else (left_other, t - own)
        lefts[pl.ds(t * half, half), :] = source[k]
    slot_of_3 = jnp.where(below_is_a(), 0, 1)
    ops = [info_own[1 + t:2 + t] if t < own else info_other[1 + t - own:2 + t - own]
           for t in range(terms)]
    factors = [[coefficient(op, p) for p in range(4)] for op in ops]
    flips = [op == FLIP for op in ops]
    rows = lax.broadcasted_iota(jnp.int32, (half, size), 0) + lax.axis_index("term") * half
    cols = lax.broadcasted_iota(jnp.int32, (half, size), 1)
    keep = jnp.maximum(rows, cols).astype(jnp.float32) < info_own[0:1]
    groups = out_sem.shape[1]
    per_group = nvec // groups
    stores = []
    for group in range(groups):
        for j in range(per_group):
            v = group * per_group + j
            loads[v].wait()
            lifted = [
                jnp.dot(lefts[...], psi_buf[v, q], preferred_element_type=jnp.float32)
                for q in range(4)
            ]
            for t in range(terms):
                part = [x[t * half:(t + 1) * half] for x in lifted]
                factor = factors[t]
                for q in (0, 3):
                    slot = slot_of_3 if q == 3 else 1 - slot_of_3
                    rim[slot, t, pl.ds(v * half, half), :] = (part[q] * factor[q]).astype(rim.dtype)
                for p in (1, 2):
                    source = jnp.where(flips[t], part[3 - p], part[p])
                    centre[p - 1, t, pl.ds(j * half, half), :] = (source * factor[p]).astype(
                        centre.dtype
                    )
        for slot in range(2):
            total = None
            for t in range(terms):
                part = times_transpose(centre[slot, t], rights[t][...])
                total = part if total is None else total + part
            for j in range(per_group):
                out_buf[slot, group * per_group + j] = jnp.where(
                    keep, total[j * half:(j + 1) * half], 0.0
                )
            vectors = pl.ds(group * per_group, per_group)
            store = pltpu.make_async_copy(
                out_buf.at[slot, vectors], sigma.at[vectors, 0, slot + 1], out_sem.at[slot, group]
            )
            store.start()
            stores.append(store)
    for store in stores:
        store.wait()


def sum_terms(rim, which, first, blocks, count, rows, total=None):
    size = rim.shape[-1]
    for k in range(count):
        product = times_transpose(rim[which, first + k, rows, :], blocks[k * size:(k + 1) * size])
        total = product if total is None else total + product
    return total


def state_mask(which, info, note, half):
    is_below = (which == 0) == below_is_a()
    me = lax.axis_index("sector")
    there = jnp.where(is_below, me, lax.axis_size("sector") - 1 - me) > 0
    shape = (half, info.shape[1])
    rows = lax.broadcasted_iota(jnp.int32, shape, 0) + lax.axis_index("term") * half
    cols = lax.broadcasted_iota(jnp.int32, shape, 1)
    keep = (rows.astype(jnp.float32) < info[0:1, :]) & there
    return keep & (cols.astype(jnp.float32) < note[0:1, :]), jnp.where(is_below, 3, 0)


def own_rim_kernel(rim, own_a, own_b, part_a, part_b):
    count, rows = own_a.shape[0] // rim.shape[-1], pl.ds(0, rim.shape[2])
    part_a[...] = sum_terms(rim, 0, 0, own_a, count, rows)
    part_b[...] = sum_terms(rim, 1, 0, own_b, count, rows)


def last_rim_kernel(info, note_a, note_b, rim, other_a, other_b, part_a, part_b, sigma_in, sigma,
                    out_buf, out_sem):
    _, nvec, half, size = out_buf.shape
    count, groups = other_a.shape[0] // size, out_sem.shape[1]
    first, per_group = rim.shape[1] - count, nvec // groups
    stores = []
    for which, note, blocks, part in ((0, note_a, other_a, part_a), (1, note_b, other_b, part_b)):
        keep, state = state_mask(which, info, note, half)
        for group in range(groups):
            rows = pl.ds(group * per_group * half, per_group * half)
            total = sum_terms(rim, which, first, blocks, count, rows, part[rows, :])
            for j in range(per_group):
                out_buf[which, group * per_group + j] = jnp.where(
                    keep, total[j * half:(j + 1) * half], 0.0
                )
            vectors = pl.ds(group * per_group, per_group)
            store = pltpu.make_async_copy(
                out_buf.at[which, vectors], sigma.at[vectors, 0, state], out_sem.at[which, group]
            )
            store.start()
            stores.append(store)
    for store in stores:
        store.wait()


def two_core_cycle(sectors):
    up = [(2 * i, 2 * i + 2) for i in range(sectors - 1)]
    down = [(2 * i + 3, 2 * i + 1) for i in range(sectors - 1)]
    return up + [(2 * sectors - 2, 2 * sectors - 1)] + down + [(1, 0)]


def shards(psi, left_env, right_env, op_index, kept_rows):
    sectors, cores = lax.axis_size("sector"), lax.axis_size("term")
    nvec, size = psi.shape[0], psi.shape[-1]
    half = size // cores
    terms = left_env.shape[0] * cores
    swap = [(0, 1), (1, 0)]

    if cores == 2:
        cycle = two_core_cycle(sectors)
        reverse = [(b, a) for a, b in cycle]
        own_a = lax.ppermute(right_env, ("sector", "term"), cycle)
        own_b = lax.ppermute(right_env, ("sector", "term"), reverse)
        info_own, left_own, left_sent, rights = pack(
            kept_rows, op_index, left_env, right_env, half
        )
        left_other = lax.ppermute(left_sent, "term", swap)
        info_other = lax.ppermute(info_own, "term", swap)
        rights += [lax.ppermute(x, "term", swap) for x in rights]
        note_a = lax.ppermute(info_own, ("sector", "term"), cycle)
    else:
        forward = [(i, i + 1) for i in range(sectors - 1)]
        backward = [(b, a) for a, b in forward]
        gathered = [lax.all_gather(x, "term", tiled=True) for x in (left_env, right_env, op_index)]
        rows = lax.dynamic_slice_in_dim(gathered[0][:, 0], lax.axis_index("term") * half, half, 1)
        left_own, left_other = jnp.split(rows, 2)
        info_own, info_other = [
            info_of(kept_rows, ops, terms // 2, size) for ops in jnp.split(gathered[2], 2)
        ]
        rights = list(gathered[1][:, 0])

        def neighbour(pairs):
            blocks = lax.all_gather(lax.ppermute(right_env, "sector", pairs), "term", tiled=True)
            return *jnp.split(blocks, 2), lax.ppermute(info_own, "sector", pairs)

        own_a, other_a, note_a = neighbour(forward)
        own_b, other_b, note_b = neighbour(backward)

    sigma_shape = jax.ShapeDtypeStruct((nvec, 1, 4, half, size), jnp.float32)
    rim_shape = jax.ShapeDtypeStruct((2, terms, nvec * half, size), jnp.bfloat16)
    part_shape = jax.ShapeDtypeStruct((nvec * half, size), jnp.float32)
    params = pltpu.CompilerParams(vmem_limit_bytes=VMEM_LIMIT)

    groups = 2 if nvec % 2 == 0 else 1
    sigma, rim = pl.pallas_call(
        centre_kernel,
        out_shape=(sigma_shape, rim_shape),
        in_specs=[HBM] + [VMEM] * (4 + terms),
        out_specs=(HBM, VMEM),
        scratch_shapes=[
            pltpu.VMEM((nvec, 4, size, size), jnp.bfloat16),
            pltpu.VMEM((terms * half, size), jnp.bfloat16),
            pltpu.VMEM((2, terms, nvec // groups * half, size), jnp.bfloat16),
            pltpu.VMEM((2, nvec, half, size), jnp.float32),
            pltpu.SemaphoreType.DMA((nvec,)),
            pltpu.SemaphoreType.DMA((2, groups)),
        ],
        compiler_params=pltpu.CompilerParams(vmem_limit_bytes=CENTRE_LIMIT),
        name="centre",
    )(psi, info_own, info_other, left_own, left_other, *rights)

    own_a, own_b, note_a, sigma, rim = lax.optimization_barrier((own_a, own_b, note_a, sigma, rim))
    if cores == 2:
        other_b = lax.ppermute(own_a, "term", swap)
        other_a = lax.ppermute(own_b, "term", swap)
        note_b = lax.ppermute(note_a, "term", swap)
    own_a, own_b, other_a, other_b = [
        x.reshape(-1, size) for x in (own_a, own_b, other_a, other_b)
    ]
    part_a, part_b = pl.pallas_call(
        own_rim_kernel,
        out_shape=(part_shape, part_shape),
        in_specs=[VMEM] * 3,
        out_specs=(VMEM, VMEM),
        compiler_params=params,
        name="own_rim",
    )(rim, own_a, own_b)
    return pl.pallas_call(
        last_rim_kernel,
        out_shape=sigma_shape,
        in_specs=[VMEM] * 8 + [HBM],
        out_specs=HBM,
        scratch_shapes=[
            pltpu.VMEM((2, nvec, half, size), jnp.float32),
            pltpu.SemaphoreType.DMA((2, groups)),
        ],
        input_output_aliases={8: 0},
        compiler_params=params,
        name="last_rim",
    )(info_own, note_a, note_b, rim, other_a, other_b, part_a, part_b, sigma)


def solution(mesh):
    in_specs = (
        P(None, "sector", None, None, None),
        P("term", "sector", None, None),
        P("term", "sector", None, None),
        P("term"),
        P("sector"),
    )
    out_specs = P(None, "sector", None, "term", None)
    return jax.shard_map(shards, mesh=mesh, in_specs=in_specs, out_specs=out_specs, check_vma=False)
```

```python
import jax
import jax.numpy as jnp
from jax import lax
from jax.experimental import pallas as pl
from jax.experimental.pallas import tpu as pltpu
from jax.sharding import PartitionSpec as P

FLIP = 2
COEFFICIENTS = (
    (1.0, 1.0, 1.0, 1.0),
    (0.25, -0.25, -0.25, 0.25),
    (0.0, 0.5, 0.5, 0.0),
    (0.5, 0.5, -0.5, -0.5),
    (0.5, -0.5, 0.5, -0.5),
)
VMEM_LIMIT = 16 * 1024 * 1024
CENTRE_LIMIT = 50 * 1024 * 1024
PACK_LIMIT = 54579 * 1024
VMEM = pl.BlockSpec(memory_space=pltpu.VMEM)
HBM = pl.BlockSpec(memory_space=pltpu.HBM)


def coefficient(op, p):
    value = jnp.full_like(op, COEFFICIENTS[-1][p])
    for kind in range(len(COEFFICIENTS) - 1):
        value = jnp.where(op == kind, COEFFICIENTS[kind][p], value)
    return value


def times_transpose(a, b):
    return lax.dot_general(a, b, (((1,), (1,)), ((), ())), preferred_element_type=jnp.float32)


def below_is_a():
    return lax.axis_index("term") == 1 if lax.axis_size("term") == 2 else True


def info_rows(terms):
    return 8 * pl.cdiv(1 + terms, 8)


def info_of(kept, ops, terms, size):
    rows = lax.broadcasted_iota(jnp.int32, (info_rows(terms), size), 0)
    info = jnp.where(rows == 0, kept[0], 0)
    for t in range(terms):
        info = jnp.where(rows == 1 + t, ops[t], info)
    return info.astype(jnp.float32)


def pack_kernel(kept, ops, left, right, info, mine, theirs, *refs):
    *blocks, kept_buf, ops_buf, sems = refs
    terms, half, size = mine.shape
    core = lax.axis_index("term")
    scalars = [
        pltpu.make_async_copy(kept, kept_buf, sems.at[0]),
        pltpu.make_async_copy(ops, ops_buf, sems.at[1]),
    ]
    copies = [
        pltpu.make_async_copy(
            left.at[:, 0, pl.ds(pl.multiple_of(who * half, half), half)], rows, sems.at[2 + k]
        )
        for k, (who, rows) in enumerate(((core, mine), (1 - core, theirs)))
    ]
    for t, block in enumerate(blocks):
        copies.append(pltpu.make_async_copy(right.at[t, 0], block, sems.at[4 + t]))
    for copy in scalars + copies:
        copy.start()
    for copy in scalars:
        copy.wait()
    info[...] = info_of(kept_buf, ops_buf, terms, size)
    for copy in copies:
        copy.wait()


def pack(kept, ops, left, right, half):
    terms, size = left.shape[0], left.shape[-1]
    rows = jax.ShapeDtypeStruct((terms, half, size), left.dtype)
    block = jax.ShapeDtypeStruct((size, size), right.dtype)
    info, mine, theirs, *blocks = pl.pallas_call(
        pack_kernel,
        out_shape=(jax.ShapeDtypeStruct((info_rows(terms), size), jnp.float32), rows, rows)
        + (block,) * terms,
        in_specs=[HBM] * 4,
        out_specs=(VMEM,) * (3 + terms),
        scratch_shapes=[
            pltpu.SMEM(kept.shape, kept.dtype),
            pltpu.SMEM(ops.shape, ops.dtype),
            pltpu.SemaphoreType.DMA((4 + terms,)),
        ],
        compiler_params=pltpu.CompilerParams(vmem_limit_bytes=PACK_LIMIT),
        name="pack",
    )(kept, ops, left, right)
    return info, mine, theirs, blocks


def centre_kernel(psi, info_own, info_other, left_own, left_other, *refs):
    (*rights, sigma, rim, psi_buf, lefts, centre, out_buf, psi_sem, out_sem) = refs
    nvec, half, size = psi.shape[0], sigma.shape[3], psi.shape[4]
    own, terms = left_own.shape[0], len(rights)
    loads = [pltpu.make_async_copy(psi.at[v, 0], psi_buf.at[v], psi_sem.at[v]) for v in range(nvec)]
    for copy in loads:
        copy.start()
    for t in range(terms):
        source, k = (left_own, t) if t < own else (left_other, t - own)
        lefts[pl.ds(t * half, half), :] = source[k]
    slot_of_3 = jnp.where(below_is_a(), 0, 1)
    ops = [info_own[1 + t:2 + t] if t < own else info_other[1 + t - own:2 + t - own]
           for t in range(terms)]
    factors = [[coefficient(op, p) for p in range(4)] for op in ops]
    flips = [op == FLIP for op in ops]
    rows = lax.broadcasted_iota(jnp.int32, (half, size), 0) + lax.axis_index("term") * half
    cols = lax.broadcasted_iota(jnp.int32, (half, size), 1)
    keep = jnp.maximum(rows, cols).astype(jnp.float32) < info_own[0:1]
    groups = out_sem.shape[1]
    per_group = nvec // groups
    stores = []
    for group in range(groups):
        for j in range(per_group):
            v = group * per_group + j
            loads[v].wait()
            lifted = [
                jnp.dot(lefts[...], psi_buf[v, q], preferred_element_type=jnp.float32)
                for q in range(4)
            ]
            for t in range(terms):
                part = [x[t * half:(t + 1) * half] for x in lifted]
                factor = factors[t]
                for q in (0, 3):
                    slot = slot_of_3 if q == 3 else 1 - slot_of_3
                    rim[slot, t, pl.ds(v * half, half), :] = (part[q] * factor[q]).astype(rim.dtype)
                for p in (1, 2):
                    source = jnp.where(flips[t], part[3 - p], part[p])
                    centre[p - 1, t, pl.ds(j * half, half), :] = (source * factor[p]).astype(
                        centre.dtype
                    )
        for slot in range(2):
            total = None
            for t in range(terms):
                part = times_transpose(centre[slot, t], rights[t][...])
                total = part if total is None else total + part
            for j in range(per_group):
                out_buf[slot, group * per_group + j] = jnp.where(
                    keep, total[j * half:(j + 1) * half], 0.0
                )
            vectors = pl.ds(group * per_group, per_group)
            store = pltpu.make_async_copy(
                out_buf.at[slot, vectors], sigma.at[vectors, 0, slot + 1], out_sem.at[slot, group]
            )
            store.start()
            stores.append(store)
    for store in stores:
        store.wait()


def sum_terms(rim, which, first, blocks, count, rows, total=None):
    size = rim.shape[-1]
    for k in range(count):
        product = times_transpose(rim[which, first + k, rows, :], blocks[k * size:(k + 1) * size])
        total = product if total is None else total + product
    return total


def state_mask(which, info, note, half):
    is_below = (which == 0) == below_is_a()
    me = lax.axis_index("sector")
    there = jnp.where(is_below, me, lax.axis_size("sector") - 1 - me) > 0
    shape = (half, info.shape[1])
    rows = lax.broadcasted_iota(jnp.int32, shape, 0) + lax.axis_index("term") * half
    cols = lax.broadcasted_iota(jnp.int32, shape, 1)
    keep = (rows.astype(jnp.float32) < info[0:1, :]) & there
    return keep & (cols.astype(jnp.float32) < note[0:1, :]), jnp.where(is_below, 3, 0)


def own_rim_kernel(rim, own_a, own_b, part_a, part_b):
    count, rows = own_a.shape[0] // rim.shape[-1], pl.ds(0, rim.shape[2])
    part_a[...] = sum_terms(rim, 0, 0, own_a, count, rows)
    part_b[...] = sum_terms(rim, 1, 0, own_b, count, rows)


def last_rim_kernel(info, note_a, note_b, rim, other_a, other_b, part_a, part_b, sigma_in, sigma,
                    out_buf, out_sem):
    _, nvec, half, size = out_buf.shape
    count, groups = other_a.shape[0] // size, out_sem.shape[1]
    first, per_group = rim.shape[1] - count, nvec // groups
    stores = []
    for which, note, blocks, part in ((0, note_a, other_a, part_a), (1, note_b, other_b, part_b)):
        keep, state = state_mask(which, info, note, half)
        for group in range(groups):
            rows = pl.ds(group * per_group * half, per_group * half)
            total = sum_terms(rim, which, first, blocks, count, rows, part[rows, :])
            for j in range(per_group):
                out_buf[which, group * per_group + j] = jnp.where(
                    keep, total[j * half:(j + 1) * half], 0.0
                )
            vectors = pl.ds(group * per_group, per_group)
            store = pltpu.make_async_copy(
                out_buf.at[which, vectors], sigma.at[vectors, 0, state], out_sem.at[which, group]
            )
            store.start()
            stores.append(store)
    for store in stores:
        store.wait()


def two_core_cycle(sectors):
    up = [(2 * i, 2 * i + 2) for i in range(sectors - 1)]
    down = [(2 * i + 3, 2 * i + 1) for i in range(sectors - 1)]
    return up + [(2 * sectors - 2, 2 * sectors - 1)] + down + [(1, 0)]


def shards(psi, left_env, right_env, op_index, kept_rows):
    sectors, cores = lax.axis_size("sector"), lax.axis_size("term")
    nvec, size = psi.shape[0], psi.shape[-1]
    half = size // cores
    terms = left_env.shape[0] * cores
    swap = [(0, 1), (1, 0)]

    if cores == 2:
        cycle = two_core_cycle(sectors)
        reverse = [(b, a) for a, b in cycle]
        own_a = lax.ppermute(right_env, ("sector", "term"), reverse)
        own_b = lax.ppermute(right_env, ("sector", "term"), cycle)
        info_own, left_own, left_sent, rights = pack(
            kept_rows, op_index, left_env, right_env, half
        )
        left_other = lax.ppermute(left_sent, "term", swap)
        info_other = lax.ppermute(info_own, "term", swap)
        rights += [lax.ppermute(x, "term", swap) for x in rights]
        note_a = lax.ppermute(info_own, ("sector", "term"), reverse)
    else:
        forward = [(i, i + 1) for i in range(sectors - 1)]
        backward = [(b, a) for a, b in forward]
        gathered = [lax.all_gather(x, "term", tiled=True) for x in (left_env, right_env, op_index)]
        rows = lax.dynamic_slice_in_dim(gathered[0][:, 0], lax.axis_index("term") * half, half, 1)
        left_own, left_other = jnp.split(rows, 2)
        info_own, info_other = [
            info_of(kept_rows, ops, terms // 2, size) for ops in jnp.split(gathered[2], 2)
        ]
        rights = list(gathered[1][:, 0])

        def neighbour(pairs):
            blocks = lax.all_gather(lax.ppermute(right_env, "sector", pairs), "term", tiled=True)
            return *jnp.split(blocks, 2), lax.ppermute(info_own, "sector", pairs)

        own_a, other_a, note_a = neighbour(forward)
        own_b, other_b, note_b = neighbour(backward)

    sigma_shape = jax.ShapeDtypeStruct((nvec, 1, 4, half, size), jnp.float32)
    rim_shape = jax.ShapeDtypeStruct((2, terms, nvec * half, size), jnp.bfloat16)
    part_shape = jax.ShapeDtypeStruct((nvec * half, size), jnp.float32)
    params = pltpu.CompilerParams(vmem_limit_bytes=VMEM_LIMIT)

    groups = 2 if nvec % 2 == 0 else 1
    sigma, rim = pl.pallas_call(
        centre_kernel,
        out_shape=(sigma_shape, rim_shape),
        in_specs=[HBM] + [VMEM] * (4 + terms),
        out_specs=(HBM, VMEM),
        scratch_shapes=[
            pltpu.VMEM((nvec, 4, size, size), jnp.bfloat16),
            pltpu.VMEM((terms * half, size), jnp.bfloat16),
            pltpu.VMEM((2, terms, nvec // groups * half, size), jnp.bfloat16),
            pltpu.VMEM((2, nvec, half, size), jnp.float32),
            pltpu.SemaphoreType.DMA((nvec,)),
            pltpu.SemaphoreType.DMA((2, groups)),
        ],
        compiler_params=pltpu.CompilerParams(vmem_limit_bytes=CENTRE_LIMIT),
        name="centre",
    )(psi, info_own, info_other, left_own, left_other, *rights)

    own_a, own_b, note_a, sigma, rim = lax.optimization_barrier((own_a, own_b, note_a, sigma, rim))
    if cores == 2:
        other_b = lax.ppermute(own_a, "term", swap)
        other_a = lax.ppermute(own_b, "term", swap)
        note_b = lax.ppermute(note_a, "term", swap)
    own_a, own_b, other_a, other_b = [
        x.reshape(-1, size) for x in (own_a, own_b, other_a, other_b)
    ]
    part_a, part_b = pl.pallas_call(
        own_rim_kernel,
        out_shape=(part_shape, part_shape),
        in_specs=[VMEM] * 3,
        out_specs=(VMEM, VMEM),
        compiler_params=params,
        name="own_rim",
    )(rim, own_a, own_b)
    return pl.pallas_call(
        last_rim_kernel,
        out_shape=sigma_shape,
        in_specs=[VMEM] * 8 + [HBM],
        out_specs=HBM,
        scratch_shapes=[
            pltpu.VMEM((2, nvec, half, size), jnp.float32),
            pltpu.SemaphoreType.DMA((2, groups)),
        ],
        input_output_aliases={8: 0},
        compiler_params=params,
        name="last_rim",
    )(info_own, note_a, note_b, rim, other_a, other_b, part_a, part_b, sigma)


def solution(mesh):
    in_specs = (
        P(None, "sector", None, None, None),
        P("term", "sector", None, None),
        P("term", "sector", None, None),
        P("term"),
        P("sector"),
    )
    out_specs = P(None, "sector", None, "term", None)
    return jax.shard_map(shards, mesh=mesh, in_specs=in_specs, out_specs=out_specs, check_vma=False)
```

```python
import jax
import jax.numpy as jnp
from jax import lax
from jax.experimental import pallas as pl
from jax.experimental.pallas import tpu as pltpu
from jax.sharding import PartitionSpec as P

FLIP = 2
COEFFICIENTS = (
    (1.0, 1.0, 1.0, 1.0),
    (0.25, -0.25, -0.25, 0.25),
    (0.0, 0.5, 0.5, 0.0),
    (0.5, 0.5, -0.5, -0.5),
    (0.5, -0.5, 0.5, -0.5),
)
VMEM_LIMIT = 16 * 1024 * 1024
CENTRE_LIMIT = 50 * 1024 * 1024
PACK_LIMIT = 54579 * 1024
VMEM = pl.BlockSpec(memory_space=pltpu.VMEM)
HBM = pl.BlockSpec(memory_space=pltpu.HBM)


def coefficient(op, p):
    value = jnp.full_like(op, COEFFICIENTS[-1][p])
    for kind in range(len(COEFFICIENTS) - 1):
        value = jnp.where(op == kind, COEFFICIENTS[kind][p], value)
    return value


def times_transpose(a, b):
    return lax.dot_general(a, b, (((1,), (1,)), ((), ())), preferred_element_type=jnp.float32)


def below_is_a():
    return lax.axis_index("sector") % 2 == 0 if lax.axis_size("term") == 2 else True


def info_rows(terms):
    return 8 * pl.cdiv(1 + terms, 8)


def info_of(kept, ops, terms, size):
    rows = lax.broadcasted_iota(jnp.int32, (info_rows(terms), size), 0)
    info = jnp.where(rows == 0, kept[0], 0)
    for t in range(terms):
        info = jnp.where(rows == 1 + t, ops[t], info)
    return info.astype(jnp.float32)


def pack_kernel(kept, ops, left, right, info, mine, theirs, *refs):
    *blocks, kept_buf, ops_buf, sems = refs
    terms, half, size = mine.shape
    core = lax.axis_index("term")
    scalars = [
        pltpu.make_async_copy(kept, kept_buf, sems.at[0]),
        pltpu.make_async_copy(ops, ops_buf, sems.at[1]),
    ]
    copies = [
        pltpu.make_async_copy(
            left.at[:, 0, pl.ds(pl.multiple_of(who * half, half), half)], rows, sems.at[2 + k]
        )
        for k, (who, rows) in enumerate(((core, mine), (1 - core, theirs)))
    ]
    for t, block in enumerate(blocks):
        copies.append(pltpu.make_async_copy(right.at[t, 0], block, sems.at[4 + t]))
    for copy in scalars + copies:
        copy.start()
    for copy in scalars:
        copy.wait()
    info[...] = info_of(kept_buf, ops_buf, terms, size)
    for copy in copies:
        copy.wait()


def pack(kept, ops, left, right, half):
    terms, size = left.shape[0], left.shape[-1]
    rows = jax.ShapeDtypeStruct((terms, half, size), left.dtype)
    block = jax.ShapeDtypeStruct((size, size), right.dtype)
    info, mine, theirs, *blocks = pl.pallas_call(
        pack_kernel,
        out_shape=(jax.ShapeDtypeStruct((info_rows(terms), size), jnp.float32), rows, rows)
        + (block,) * terms,
        in_specs=[HBM] * 4,
        out_specs=(VMEM,) * (3 + terms),
        scratch_shapes=[
            pltpu.SMEM(kept.shape, kept.dtype),
            pltpu.SMEM(ops.shape, ops.dtype),
            pltpu.SemaphoreType.DMA((4 + terms,)),
        ],
        compiler_params=pltpu.CompilerParams(vmem_limit_bytes=PACK_LIMIT),
        name="pack",
    )(kept, ops, left, right)
    return info, mine, theirs, blocks


def centre_kernel(psi, info_own, info_other, left_own, left_other, *refs):
    (*rights, sigma, rim, psi_buf, lefts, centre, out_buf, psi_sem, out_sem) = refs
    nvec, half, size = psi.shape[0], sigma.shape[3], psi.shape[4]
    own, terms = left_own.shape[0], len(rights)
    loads = [pltpu.make_async_copy(psi.at[v, 0], psi_buf.at[v], psi_sem.at[v]) for v in range(nvec)]
    for copy in loads:
        copy.start()
    for t in range(terms):
        source, k = (left_own, t) if t < own else (left_other, t - own)
        lefts[pl.ds(t * half, half), :] = source[k]
    slot_of_3 = jnp.where(below_is_a(), 0, 1)
    ops = [info_own[1 + t:2 + t] if t < own else info_other[1 + t - own:2 + t - own]
           for t in range(terms)]
    factors = [[coefficient(op, p) for p in range(4)] for op in ops]
    flips = [op == FLIP for op in ops]
    rows = lax.broadcasted_iota(jnp.int32, (half, size), 0) + lax.axis_index("term") * half
    cols = lax.broadcasted_iota(jnp.int32, (half, size), 1)
    keep = jnp.maximum(rows, cols).astype(jnp.float32) < info_own[0:1]
    groups = out_sem.shape[1]
    per_group = nvec // groups
    stores = []
    for group in range(groups):
        for j in range(per_group):
            v = group * per_group + j
            loads[v].wait()
            lifted = [
                jnp.dot(lefts[...], psi_buf[v, q], preferred_element_type=jnp.float32)
                for q in range(4)
            ]
            for t in range(terms):
                part = [x[t * half:(t + 1) * half] for x in lifted]
                factor = factors[t]
                for q in (0, 3):
                    slot = slot_of_3 if q == 3 else 1 - slot_of_3
                    rim[slot, t, pl.ds(v * half, half), :] = (part[q] * factor[q]).astype(rim.dtype)
                for p in (1, 2):
                    source = jnp.where(flips[t], part[3 - p], part[p])
                    centre[p - 1, t, pl.ds(j * half, half), :] = (source * factor[p]).astype(
                        centre.dtype
                    )
        for slot in range(2):
            total = None
            for t in range(terms):
                part = times_transpose(centre[slot, t], rights[t][...])
                total = part if total is None else total + part
            for j in range(per_group):
                out_buf[slot, group * per_group + j] = jnp.where(
                    keep, total[j * half:(j + 1) * half], 0.0
                )
            vectors = pl.ds(group * per_group, per_group)
            store = pltpu.make_async_copy(
                out_buf.at[slot, vectors], sigma.at[vectors, 0, slot + 1], out_sem.at[slot, group]
            )
            store.start()
            stores.append(store)
    for store in stores:
        store.wait()


def sum_terms(rim, which, first, blocks, count, rows, total=None):
    size = rim.shape[-1]
    for k in range(count):
        product = times_transpose(rim[which, first + k, rows, :], blocks[k * size:(k + 1) * size])
        total = product if total is None else total + product
    return total


def state_mask(which, info, note, half):
    is_below = (which == 0) == below_is_a()
    me = lax.axis_index("sector")
    there = jnp.where(is_below, me, lax.axis_size("sector") - 1 - me) > 0
    shape = (half, info.shape[1])
    rows = lax.broadcasted_iota(jnp.int32, shape, 0) + lax.axis_index("term") * half
    cols = lax.broadcasted_iota(jnp.int32, shape, 1)
    keep = (rows.astype(jnp.float32) < info[0:1, :]) & there
    return keep & (cols.astype(jnp.float32) < note), jnp.where(is_below, 3, 0)


def middle_kernel(rim, own_a, own_b, other_b, part_a, part_b):
    own, other = own_b.shape[0] // rim.shape[-1], other_b.shape[0] // rim.shape[-1]
    rows = pl.ds(0, rim.shape[2])
    part_b[...] = sum_terms(
        rim, 1, own, other_b, other, rows, sum_terms(rim, 1, 0, own_b, own, rows)
    )
    part_a[...] = sum_terms(rim, 0, 0, own_a, own, rows)


def last_kernel(info, note, note_other, rim, other_a, part_a, part_b, sigma_in, sigma, out_buf, out_sem):
    _, nvec, half, size = out_buf.shape
    count, groups = other_a.shape[0] // size, out_sem.shape[1]
    first, per_group = rim.shape[1] - count, nvec // groups
    direct = (lax.axis_index("term") == 0) == below_is_a()
    notes = note[0:1, :], note_other[0:1, :]
    note_a, note_b = jnp.where(direct, *notes), jnp.where(direct, *notes[::-1])
    stores = []
    for which, note, part in ((1, note_b, part_b), (0, note_a, part_a)):
        keep, state = state_mask(which, info, note, half)
        for group in range(groups):
            rows = pl.ds(group * per_group * half, per_group * half)
            total = part[rows, :]
            if which == 0:
                total = sum_terms(rim, 0, first, other_a, count, rows, total)
            for j in range(per_group):
                out_buf[which, group * per_group + j] = jnp.where(
                    keep, total[j * half:(j + 1) * half], 0.0
                )
            vectors = pl.ds(group * per_group, per_group)
            store = pltpu.make_async_copy(
                out_buf.at[which, vectors], sigma.at[vectors, 0, state], out_sem.at[which, group]
            )
            store.start()
            stores.append(store)
    for store in stores:
        store.wait()


def two_core_cycle(sectors):
    up = [(2 * i, 2 * i + 2) for i in range(sectors - 1)]
    down = [(2 * i + 3, 2 * i + 1) for i in range(sectors - 1)]
    return up + [(2 * sectors - 2, 2 * sectors - 1)] + down + [(1, 0)]


def pair_exchange(sectors, first):
    pairs = []
    for sector in range(sectors):
        low = sector if (sector - first) % 2 == 0 else sector - 1
        alone = low < 0 or low + 1 >= sectors
        for core in range(2):
            target = 2 * sector + 1 - core if alone else 2 * (2 * low + 1 - sector) + core
            pairs.append((2 * sector + core, target))
    return pairs


def shards(psi, left_env, right_env, op_index, kept_rows):
    sectors, cores = lax.axis_size("sector"), lax.axis_size("term")
    nvec, size = psi.shape[0], psi.shape[-1]
    half = size // cores
    terms = left_env.shape[0] * cores
    swap = [(0, 1), (1, 0)]

    if cores == 2:
        cycle = two_core_cycle(sectors)
        own_b = lax.ppermute(right_env, ("sector", "term"), pair_exchange(sectors, 0))
        own_a = lax.ppermute(right_env, ("sector", "term"), pair_exchange(sectors, 1))
        info_own, left_own, left_sent, rights = pack(
            kept_rows, op_index, left_env, right_env, half
        )
        left_other = lax.ppermute(left_sent, "term", swap)
        info_other = lax.ppermute(info_own, "term", swap)
        rights += [lax.ppermute(x, "term", swap) for x in rights]
        note = lax.ppermute(info_own, ("sector", "term"), cycle)
    else:
        forward = [(i, i + 1) for i in range(sectors - 1)]
        backward = [(b, a) for a, b in forward]
        gathered = [lax.all_gather(x, "term", tiled=True) for x in (left_env, right_env, op_index)]
        rows = lax.dynamic_slice_in_dim(gathered[0][:, 0], lax.axis_index("term") * half, half, 1)
        left_own, left_other = jnp.split(rows, 2)
        info_own, info_other = [
            info_of(kept_rows, ops, terms // 2, size) for ops in jnp.split(gathered[2], 2)
        ]
        rights = list(gathered[1][:, 0])

        def neighbour(pairs):
            blocks = lax.all_gather(lax.ppermute(right_env, "sector", pairs), "term", tiled=True)
            return *jnp.split(blocks, 2), lax.ppermute(info_own, "sector", pairs)

        own_a, other_a, note = neighbour(forward)
        own_b, other_b, note_other = neighbour(backward)

    sigma_shape = jax.ShapeDtypeStruct((nvec, 1, 4, half, size), jnp.float32)
    rim_shape = jax.ShapeDtypeStruct((2, terms, nvec * half, size), jnp.bfloat16)
    part_shape = jax.ShapeDtypeStruct((nvec * half, size), jnp.float32)
    params = pltpu.CompilerParams(vmem_limit_bytes=VMEM_LIMIT)

    groups = 2 if nvec % 2 == 0 else 1
    sigma, rim = pl.pallas_call(
        centre_kernel,
        out_shape=(sigma_shape, rim_shape),
        in_specs=[HBM] + [VMEM] * (4 + terms),
        out_specs=(HBM, VMEM),
        scratch_shapes=[
            pltpu.VMEM((nvec, 4, size, size), jnp.bfloat16),
            pltpu.VMEM((terms * half, size), jnp.bfloat16),
            pltpu.VMEM((2, terms, nvec // groups * half, size), jnp.bfloat16),
            pltpu.VMEM((2, nvec, half, size), jnp.float32),
            pltpu.SemaphoreType.DMA((nvec,)),
            pltpu.SemaphoreType.DMA((2, groups)),
        ],
        compiler_params=pltpu.CompilerParams(vmem_limit_bytes=CENTRE_LIMIT),
        name="centre",
    )(psi, info_own, info_other, left_own, left_other, *rights)

    own_a, own_b = own_a.reshape(-1, size), own_b.reshape(-1, size)
    own_b, sigma, rim = lax.optimization_barrier((own_b, sigma, rim))
    own_a, note, sigma = lax.optimization_barrier((own_a, note, sigma))
    if cores == 2:
        other_b = lax.ppermute(own_b, "term", swap)
        other_a = lax.ppermute(own_a, "term", swap)
        note_other = lax.ppermute(note, "term", swap)
    part_a, part_b = pl.pallas_call(
        middle_kernel,
        out_shape=(part_shape, part_shape),
        in_specs=[VMEM] * 4,
        out_specs=(VMEM, VMEM),
        compiler_params=params,
        name="middle",
    )(rim, own_a, own_b, other_b.reshape(-1, size))
    return pl.pallas_call(
        last_kernel,
        out_shape=sigma_shape,
        in_specs=[VMEM] * 7 + [HBM],
        out_specs=HBM,
        scratch_shapes=[
            pltpu.VMEM((2, nvec, half, size), jnp.float32),
            pltpu.SemaphoreType.DMA((2, groups)),
        ],
        input_output_aliases={7: 0},
        compiler_params=params,
        name="last",
    )(info_own, note, note_other, rim, other_a.reshape(-1, size), part_a, part_b, sigma)


def solution(mesh):
    in_specs = (
        P(None, "sector", None, None, None),
        P("term", "sector", None, None),
        P("term", "sector", None, None),
        P("term"),
        P("sector"),
    )
    out_specs = P(None, "sector", None, "term", None)
    return jax.shard_map(shards, mesh=mesh, in_specs=in_specs, out_specs=out_specs, check_vma=False)
```

```python
import jax
import jax.numpy as jnp
from jax import lax
from jax.experimental import pallas as pl
from jax.experimental.pallas import tpu as pltpu
from jax.sharding import PartitionSpec as P

FLIP = 2
COEFFICIENTS = (
    (1.0, 1.0, 1.0, 1.0),
    (0.25, -0.25, -0.25, 0.25),
    (0.0, 0.5, 0.5, 0.0),
    (0.5, 0.5, -0.5, -0.5),
    (0.5, -0.5, 0.5, -0.5),
)
VMEM_LIMIT = 16 * 1024 * 1024
CENTRE_LIMIT = 50 * 1024 * 1024
PACK_LIMIT = 54579 * 1024
VMEM = pl.BlockSpec(memory_space=pltpu.VMEM)
HBM = pl.BlockSpec(memory_space=pltpu.HBM)


def coefficient(op, p):
    value = jnp.full_like(op, COEFFICIENTS[-1][p])
    for kind in range(len(COEFFICIENTS) - 1):
        value = jnp.where(op == kind, COEFFICIENTS[kind][p], value)
    return value


def times_transpose(a, b):
    return lax.dot_general(a, b, (((1,), (1,)), ((), ())), preferred_element_type=jnp.float32)


def below_is_a():
    return lax.axis_index("sector") % 2 == 0 if lax.axis_size("term") == 2 else True


def info_rows(terms):
    return 8 * pl.cdiv(1 + terms, 8)


def info_of(kept, ops, terms, size):
    rows = lax.broadcasted_iota(jnp.int32, (info_rows(terms), size), 0)
    info = jnp.where(rows == 0, kept[0], 0)
    for t in range(terms):
        info = jnp.where(rows == 1 + t, ops[t], info)
    return info.astype(jnp.float32)


def pack_kernel(kept, ops, left, right, info, mine, theirs, *refs):
    *blocks, kept_buf, ops_buf, sems = refs
    terms, half, size = mine.shape
    core = lax.axis_index("term")
    scalars = [
        pltpu.make_async_copy(kept, kept_buf, sems.at[0]),
        pltpu.make_async_copy(ops, ops_buf, sems.at[1]),
    ]
    copies = [
        pltpu.make_async_copy(
            left.at[:, 0, pl.ds(pl.multiple_of(who * half, half), half)], rows, sems.at[2 + k]
        )
        for k, (who, rows) in enumerate(((core, mine), (1 - core, theirs)))
    ]
    for t, block in enumerate(blocks):
        copies.append(pltpu.make_async_copy(right.at[t, 0], block, sems.at[4 + t]))
    for copy in scalars + copies:
        copy.start()
    for copy in scalars:
        copy.wait()
    info[...] = info_of(kept_buf, ops_buf, terms, size)
    for copy in copies:
        copy.wait()


def pack(kept, ops, left, right, half):
    terms, size = left.shape[0], left.shape[-1]
    rows = jax.ShapeDtypeStruct((terms, half, size), left.dtype)
    block = jax.ShapeDtypeStruct((size, size), right.dtype)
    info, mine, theirs, *blocks = pl.pallas_call(
        pack_kernel,
        out_shape=(jax.ShapeDtypeStruct((info_rows(terms), size), jnp.float32), rows, rows)
        + (block,) * terms,
        in_specs=[HBM] * 4,
        out_specs=(VMEM,) * (3 + terms),
        scratch_shapes=[
            pltpu.SMEM(kept.shape, kept.dtype),
            pltpu.SMEM(ops.shape, ops.dtype),
            pltpu.SemaphoreType.DMA((4 + terms,)),
        ],
        compiler_params=pltpu.CompilerParams(vmem_limit_bytes=PACK_LIMIT),
        name="pack",
    )(kept, ops, left, right)
    return info, mine, theirs, blocks


def centre_kernel(psi, info_own, info_other, left_own, left_other, *refs):
    (*rights, sigma, rim, psi_buf, lefts, centre, out_buf, psi_sem, out_sem) = refs
    nvec, half, size = psi.shape[0], sigma.shape[3], psi.shape[4]
    own, terms = left_own.shape[0], len(rights)
    loads = [pltpu.make_async_copy(psi.at[v, 0], psi_buf.at[v], psi_sem.at[v]) for v in range(nvec)]
    for copy in loads:
        copy.start()
    for t in range(terms):
        source, k = (left_own, t) if t < own else (left_other, t - own)
        lefts[pl.ds(t * half, half), :] = source[k]
    slot_of_3 = jnp.where(below_is_a(), 0, 1)
    ops = [info_own[1 + t:2 + t] if t < own else info_other[1 + t - own:2 + t - own]
           for t in range(terms)]
    factors = [[coefficient(op, p) for p in range(4)] for op in ops]
    flips = [op == FLIP for op in ops]
    rows = lax.broadcasted_iota(jnp.int32, (half, size), 0) + lax.axis_index("term") * half
    cols = lax.broadcasted_iota(jnp.int32, (half, size), 1)
    keep = jnp.maximum(rows, cols).astype(jnp.float32) < info_own[0:1]
    groups = out_sem.shape[1]
    per_group = nvec // groups
    stores = []
    for group in range(groups):
        for j in range(per_group):
            v = group * per_group + j
            loads[v].wait()
            lifted = [
                jnp.dot(lefts[...], psi_buf[v, q], preferred_element_type=jnp.float32)
                for q in range(4)
            ]
            for t in range(terms):
                part = [x[t * half:(t + 1) * half] for x in lifted]
                factor = factors[t]
                for q in (0, 3):
                    slot = slot_of_3 if q == 3 else 1 - slot_of_3
                    rim[slot, t, pl.ds(v * half, half), :] = (part[q] * factor[q]).astype(rim.dtype)
                for p in (1, 2):
                    source = jnp.where(flips[t], part[3 - p], part[p])
                    centre[p - 1, t, pl.ds(j * half, half), :] = (source * factor[p]).astype(
                        centre.dtype
                    )
        for slot in range(2):
            total = None
            for t in range(terms):
                part = times_transpose(centre[slot, t], rights[t][...])
                total = part if total is None else total + part
            for j in range(per_group):
                out_buf[slot, group * per_group + j] = jnp.where(
                    keep, total[j * half:(j + 1) * half], 0.0
                )
            vectors = pl.ds(group * per_group, per_group)
            store = pltpu.make_async_copy(
                out_buf.at[slot, vectors], sigma.at[vectors, 0, slot + 1], out_sem.at[slot, group]
            )
            store.start()
            stores.append(store)
    for store in stores:
        store.wait()


def sum_terms(rim, which, first, blocks, count, rows, total=None):
    size = rim.shape[-1]
    for k in range(count):
        product = times_transpose(rim[which, first + k, rows, :], blocks[k * size:(k + 1) * size])
        total = product if total is None else total + product
    return total


def state_mask(which, info, note, half):
    is_below = (which == 0) == below_is_a()
    me = lax.axis_index("sector")
    there = jnp.where(is_below, me, lax.axis_size("sector") - 1 - me) > 0
    shape = (half, info.shape[1])
    rows = lax.broadcasted_iota(jnp.int32, shape, 0) + lax.axis_index("term") * half
    cols = lax.broadcasted_iota(jnp.int32, shape, 1)
    keep = (rows.astype(jnp.float32) < info[0:1, :]) & there
    return keep & (cols.astype(jnp.float32) < note), jnp.where(is_below, 3, 0)


def middle_kernel(rim, own_a, own_b, other_b, part_a, part_b):
    own, other = own_b.shape[0] // rim.shape[-1], other_b.shape[0] // rim.shape[-1]
    rows = pl.ds(0, rim.shape[2])
    part_b[...] = sum_terms(
        rim, 1, own, other_b, other, rows, sum_terms(rim, 1, 0, own_b, own, rows)
    )
    part_a[...] = sum_terms(rim, 0, 0, own_a, own, rows)


def last_kernel(info, note, note_other, rim, other_a, part_a, part_b, sigma_in, sigma, out_buf, out_sem):
    _, nvec, half, size = out_buf.shape
    count, groups = other_a.shape[0] // size, out_sem.shape[1]
    first, per_group = rim.shape[1] - count, nvec // groups
    direct = (lax.axis_index("term") == 0) == below_is_a() if lax.axis_size("term") == 2 else True
    notes = note[0:1, :], note_other[0:1, :]
    note_a, note_b = jnp.where(direct, *notes), jnp.where(direct, *notes[::-1])
    stores = []
    for which, note, part in ((1, note_b, part_b), (0, note_a, part_a)):
        keep, state = state_mask(which, info, note, half)
        for group in range(groups):
            rows = pl.ds(group * per_group * half, per_group * half)
            total = part[rows, :]
            if which == 0:
                total = sum_terms(rim, 0, first, other_a, count, rows, total)
            for j in range(per_group):
                out_buf[which, group * per_group + j] = jnp.where(
                    keep, total[j * half:(j + 1) * half], 0.0
                )
            vectors = pl.ds(group * per_group, per_group)
            store = pltpu.make_async_copy(
                out_buf.at[which, vectors], sigma.at[vectors, 0, state], out_sem.at[which, group]
            )
            store.start()
            stores.append(store)
    for store in stores:
        store.wait()


def two_core_cycle(sectors):
    up = [(2 * i, 2 * i + 2) for i in range(sectors - 1)]
    down = [(2 * i + 3, 2 * i + 1) for i in range(sectors - 1)]
    return up + [(2 * sectors - 2, 2 * sectors - 1)] + down + [(1, 0)]


def pair_exchange(sectors, first):
    pairs = []
    for sector in range(sectors):
        low = sector if (sector - first) % 2 == 0 else sector - 1
        alone = low < 0 or low + 1 >= sectors
        for core in range(2):
            target = 2 * sector + 1 - core if alone else 2 * (2 * low + 1 - sector) + core
            pairs.append((2 * sector + core, target))
    return pairs


def shards(psi, left_env, right_env, op_index, kept_rows):
    sectors, cores = lax.axis_size("sector"), lax.axis_size("term")
    nvec, size = psi.shape[0], psi.shape[-1]
    half = size // cores
    terms = left_env.shape[0] * cores
    swap = [(0, 1), (1, 0)]

    if cores == 2:
        cycle = two_core_cycle(sectors)
        own_b = lax.ppermute(right_env, ("sector", "term"), pair_exchange(sectors, 0))
        own_a = lax.ppermute(right_env, ("sector", "term"), pair_exchange(sectors, 1))
        info_own, left_own, left_sent, rights = pack(
            kept_rows, op_index, left_env, right_env, half
        )
        left_other = lax.ppermute(left_sent, "term", swap)
        info_other = lax.ppermute(info_own, "term", swap)
        rights += [lax.ppermute(x, "term", swap) for x in rights]
        note = lax.ppermute(info_own, ("sector", "term"), cycle)
    else:
        forward = [(i, i + 1) for i in range(sectors - 1)]
        backward = [(b, a) for a, b in forward]
        gathered = [lax.all_gather(x, "term", tiled=True) for x in (left_env, right_env, op_index)]
        rows = lax.dynamic_slice_in_dim(gathered[0][:, 0], lax.axis_index("term") * half, half, 1)
        left_own, left_other = jnp.split(rows, 2)
        info_own, info_other = [
            info_of(kept_rows, ops, terms // 2, size) for ops in jnp.split(gathered[2], 2)
        ]
        rights = list(gathered[1][:, 0])

        def neighbour(pairs):
            blocks = lax.all_gather(lax.ppermute(right_env, "sector", pairs), "term", tiled=True)
            return *jnp.split(blocks, 2), lax.ppermute(info_own, "sector", pairs)

        own_a, other_a, note = neighbour(forward)
        own_b, other_b, note_other = neighbour(backward)

    sigma_shape = jax.ShapeDtypeStruct((nvec, 1, 4, half, size), jnp.float32)
    rim_shape = jax.ShapeDtypeStruct((2, terms, nvec * half, size), jnp.bfloat16)
    part_shape = jax.ShapeDtypeStruct((nvec * half, size), jnp.float32)
    params = pltpu.CompilerParams(vmem_limit_bytes=VMEM_LIMIT)

    groups = 2 if nvec % 2 == 0 else 1
    sigma, rim = pl.pallas_call(
        centre_kernel,
        out_shape=(sigma_shape, rim_shape),
        in_specs=[HBM] + [VMEM] * (4 + terms),
        out_specs=(HBM, VMEM),
        scratch_shapes=[
            pltpu.VMEM((nvec, 4, size, size), jnp.bfloat16),
            pltpu.VMEM((terms * half, size), jnp.bfloat16),
            pltpu.VMEM((2, terms, nvec // groups * half, size), jnp.bfloat16),
            pltpu.VMEM((2, nvec, half, size), jnp.float32),
            pltpu.SemaphoreType.DMA((nvec,)),
            pltpu.SemaphoreType.DMA((2, groups)),
        ],
        compiler_params=pltpu.CompilerParams(vmem_limit_bytes=CENTRE_LIMIT),
        name="centre",
    )(psi, info_own, info_other, left_own, left_other, *rights)

    own_a, own_b = own_a.reshape(-1, size), own_b.reshape(-1, size)
    own_b, sigma, rim = lax.optimization_barrier((own_b, sigma, rim))
    own_a, note, sigma = lax.optimization_barrier((own_a, note, sigma))
    if cores == 2:
        other_b = lax.ppermute(own_b, "term", swap)
        other_a = lax.ppermute(own_a, "term", swap)
        note_other = lax.ppermute(note, "term", swap)
    part_a, part_b = pl.pallas_call(
        middle_kernel,
        out_shape=(part_shape, part_shape),
        in_specs=[VMEM] * 4,
        out_specs=(VMEM, VMEM),
        compiler_params=params,
        name="middle",
    )(rim, own_a, own_b, other_b.reshape(-1, size))
    return pl.pallas_call(
        last_kernel,
        out_shape=sigma_shape,
        in_specs=[VMEM] * 7 + [HBM],
        out_specs=HBM,
        scratch_shapes=[
            pltpu.VMEM((2, nvec, half, size), jnp.float32),
            pltpu.SemaphoreType.DMA((2, groups)),
        ],
        input_output_aliases={7: 0},
        compiler_params=params,
        name="last",
    )(info_own, note, note_other, rim, other_a.reshape(-1, size), part_a, part_b, sigma)


def solution(mesh):
    in_specs = (
        P(None, "sector", None, None, None),
        P("term", "sector", None, None),
        P("term", "sector", None, None),
        P("term"),
        P("sector"),
    )
    out_specs = P(None, "sector", None, "term", None)
    return jax.shard_map(shards, mesh=mesh, in_specs=in_specs, out_specs=out_specs, check_vma=False)
```

```python
import jax
import jax.numpy as jnp
from jax import lax
from jax.experimental import pallas as pl
from jax.experimental.pallas import tpu as pltpu
from jax.sharding import PartitionSpec as P

FLIP = 2
NOTE = 128
COEFFICIENTS = (
    (1.0, 1.0, 1.0, 1.0),
    (0.25, -0.25, -0.25, 0.25),
    (0.0, 0.5, 0.5, 0.0),
    (0.5, 0.5, -0.5, -0.5),
    (0.5, -0.5, 0.5, -0.5),
)
VMEM_LIMIT = 16 * 1024 * 1024
CENTRE_LIMIT = 50 * 1024 * 1024
PACK_LIMIT = 54579 * 1024
VMEM = pl.BlockSpec(memory_space=pltpu.VMEM)
HBM = pl.BlockSpec(memory_space=pltpu.HBM)


def coefficient(op, p):
    value = jnp.full_like(op, COEFFICIENTS[-1][p])
    for kind in range(len(COEFFICIENTS) - 1):
        value = jnp.where(op == kind, COEFFICIENTS[kind][p], value)
    return value


def times_transpose(a, b):
    return lax.dot_general(a, b, (((1,), (1,)), ((), ())), preferred_element_type=jnp.float32)


def below_is_a():
    return lax.axis_index("sector") % 2 == 0 if lax.axis_size("term") == 2 else True


def info_rows(terms):
    return 8 * pl.cdiv(1 + terms, 8)


def info_of(kept, ops, terms, size):
    rows = lax.broadcasted_iota(jnp.int32, (info_rows(terms), size), 0)
    info = jnp.where(rows == 0, kept[0], 0)
    for t in range(terms):
        info = jnp.where(rows == 1 + t, ops[t], info)
    return info.astype(jnp.float32)


def pack_kernel(kept, ops, left, right, info, note, mine, theirs, *refs):
    *blocks, kept_buf, ops_buf, sems = refs
    terms, half, size = mine.shape
    core = lax.axis_index("term")
    scalars = [
        pltpu.make_async_copy(kept, kept_buf, sems.at[0]),
        pltpu.make_async_copy(ops, ops_buf, sems.at[1]),
    ]
    copies = [
        pltpu.make_async_copy(
            left.at[:, 0, pl.ds(pl.multiple_of(who * half, half), half)], rows, sems.at[2 + k]
        )
        for k, (who, rows) in enumerate(((core, mine), (1 - core, theirs)))
    ]
    for t, block in enumerate(blocks):
        copies.append(pltpu.make_async_copy(right.at[t, 0], block, sems.at[4 + t]))
    for copy in scalars + copies:
        copy.start()
    for copy in scalars:
        copy.wait()
    info[...] = info_of(kept_buf, ops_buf, terms, size)
    note[...] = info[0:8, 0:NOTE]
    for copy in copies:
        copy.wait()


def pack(kept, ops, left, right, half):
    terms, size = left.shape[0], left.shape[-1]
    rows = jax.ShapeDtypeStruct((terms, half, size), left.dtype)
    block = jax.ShapeDtypeStruct((size, size), right.dtype)
    info, note, mine, theirs, *blocks = pl.pallas_call(
        pack_kernel,
        out_shape=(jax.ShapeDtypeStruct((info_rows(terms), size), jnp.float32),
                   jax.ShapeDtypeStruct((8, NOTE), jnp.float32), rows, rows)
        + (block,) * terms,
        in_specs=[HBM] * 4,
        out_specs=(VMEM,) * (4 + terms),
        scratch_shapes=[
            pltpu.SMEM(kept.shape, kept.dtype),
            pltpu.SMEM(ops.shape, ops.dtype),
            pltpu.SemaphoreType.DMA((4 + terms,)),
        ],
        compiler_params=pltpu.CompilerParams(vmem_limit_bytes=PACK_LIMIT),
        name="pack",
    )(kept, ops, left, right)
    return info, note, mine, theirs, blocks


def centre_kernel(psi, info_own, info_other, left_own, left_other, *refs):
    (*rights, sigma, rim, psi_buf, lefts, centre, out_buf, psi_sem, out_sem) = refs
    nvec, half, size = psi.shape[0], sigma.shape[3], psi.shape[4]
    own, terms = left_own.shape[0], len(rights)
    loads = [pltpu.make_async_copy(psi.at[v, 0], psi_buf.at[v], psi_sem.at[v]) for v in range(nvec)]
    for copy in loads:
        copy.start()
    for t in range(terms):
        source, k = (left_own, t) if t < own else (left_other, t - own)
        lefts[pl.ds(t * half, half), :] = source[k]
    slot_of_3 = jnp.where(below_is_a(), 0, 1)
    ops = [info_own[1 + t:2 + t] if t < own else info_other[1 + t - own:2 + t - own]
           for t in range(terms)]
    factors = [[coefficient(op, p) for p in range(4)] for op in ops]
    flips = [op == FLIP for op in ops]
    rows = lax.broadcasted_iota(jnp.int32, (half, size), 0) + lax.axis_index("term") * half
    cols = lax.broadcasted_iota(jnp.int32, (half, size), 1)
    keep = jnp.maximum(rows, cols).astype(jnp.float32) < info_own[0:1]
    groups = out_sem.shape[1]
    per_group = nvec // groups
    stores = []
    for group in range(groups):
        for j in range(per_group):
            v = group * per_group + j
            loads[v].wait()
            lifted = [
                jnp.dot(lefts[...], psi_buf[v, q], preferred_element_type=jnp.float32)
                for q in range(4)
            ]
            for t in range(terms):
                part = [x[t * half:(t + 1) * half] for x in lifted]
                factor = factors[t]
                for q in (0, 3):
                    slot = slot_of_3 if q == 3 else 1 - slot_of_3
                    rim[slot, t, pl.ds(v * half, half), :] = (part[q] * factor[q]).astype(rim.dtype)
                for p in (1, 2):
                    source = jnp.where(flips[t], part[3 - p], part[p])
                    centre[p - 1, t, pl.ds(j * half, half), :] = (source * factor[p]).astype(
                        centre.dtype
                    )
        for slot in range(2):
            total = None
            for t in range(terms):
                part = times_transpose(centre[slot, t], rights[t][...])
                total = part if total is None else total + part
            for j in range(per_group):
                out_buf[slot, group * per_group + j] = jnp.where(
                    keep, total[j * half:(j + 1) * half], 0.0
                )
            vectors = pl.ds(group * per_group, per_group)
            store = pltpu.make_async_copy(
                out_buf.at[slot, vectors], sigma.at[vectors, 0, slot + 1], out_sem.at[slot, group]
            )
            store.start()
            stores.append(store)
    for store in stores:
        store.wait()


def sum_terms(rim, which, first, blocks, count, rows, total=None):
    size = rim.shape[-1]
    for k in range(count):
        product = times_transpose(rim[which, first + k, rows, :], blocks[k * size:(k + 1) * size])
        total = product if total is None else total + product
    return total


def state_mask(which, info, note, half):
    is_below = (which == 0) == below_is_a()
    me = lax.axis_index("sector")
    there = jnp.where(is_below, me, lax.axis_size("sector") - 1 - me) > 0
    shape = (half, info.shape[1])
    rows = lax.broadcasted_iota(jnp.int32, shape, 0) + lax.axis_index("term") * half
    cols = lax.broadcasted_iota(jnp.int32, shape, 1)
    keep = (rows.astype(jnp.float32) < info[0:1, :]) & there
    return keep & (cols.astype(jnp.float32) < note), jnp.where(is_below, 3, 0)


def crossed():
    return lax.axis_size("term") == 2


def own_kernel(rim, own_a, own_b, part_a, part_b):
    count, rows = own_b.shape[0] // rim.shape[-1], pl.ds(0, rim.shape[2])
    part_a[...] = sum_terms(rim, 0, count if crossed() else 0, own_a, count, rows)
    part_b[...] = sum_terms(rim, 1, 0, own_b, count, rows)


def other_kernel(rim, other_b, part_in, part_b):
    count, rows = other_b.shape[0] // rim.shape[-1], pl.ds(0, rim.shape[2])
    part_b[...] = sum_terms(rim, 1, rim.shape[1] - count, other_b, count, rows, part_in[...])


def last_kernel(info, note, note_other, rim, other_a, part_a, part_b, sigma_in, sigma, out_buf, out_sem):
    _, nvec, half, size = out_buf.shape
    count, groups = other_a.shape[0] // size, out_sem.shape[1]
    first, per_group = 0 if crossed() else rim.shape[1] - count, nvec // groups
    direct = (lax.axis_index("term") == 0) == below_is_a() if lax.axis_size("term") == 2 else True
    notes = [jnp.concatenate([x[0:1, :]] * (size // NOTE), 1) for x in (note, note_other)]
    note_a, note_b = jnp.where(direct, *notes), jnp.where(direct, *notes[::-1])
    stores = []
    for which, note, part in ((1, note_b, part_b), (0, note_a, part_a)):
        keep, state = state_mask(which, info, note, half)
        for group in range(groups):
            rows = pl.ds(group * per_group * half, per_group * half)
            total = part[rows, :]
            if which == 0:
                total = sum_terms(rim, 0, first, other_a, count, rows, total)
            for j in range(per_group):
                out_buf[which, group * per_group + j] = jnp.where(
                    keep, total[j * half:(j + 1) * half], 0.0
                )
            vectors = pl.ds(group * per_group, per_group)
            store = pltpu.make_async_copy(
                out_buf.at[which, vectors], sigma.at[vectors, 0, state], out_sem.at[which, group]
            )
            store.start()
            stores.append(store)
    for store in stores:
        store.wait()


def two_core_cycle(sectors):
    up = [(2 * i, 2 * i + 2) for i in range(sectors - 1)]
    down = [(2 * i + 3, 2 * i + 1) for i in range(sectors - 1)]
    return up + [(2 * sectors - 2, 2 * sectors - 1)] + down + [(1, 0)]


def pair_exchange(sectors, first, cross):
    pairs = []
    for sector in range(sectors):
        low = sector if (sector - first) % 2 == 0 else sector - 1
        alone = low < 0 or low + 1 >= sectors
        for core in range(2):
            target = 2 * sector + 1 - core if alone else 2 * (2 * low + 1 - sector) + (core ^ cross)
            pairs.append((2 * sector + core, target))
    return pairs


def shards(psi, left_env, right_env, op_index, kept_rows):
    sectors, cores = lax.axis_size("sector"), lax.axis_size("term")
    nvec, size = psi.shape[0], psi.shape[-1]
    half = size // cores
    terms = left_env.shape[0] * cores
    swap = [(0, 1), (1, 0)]

    if cores == 2:
        cycle = two_core_cycle(sectors)
        own_b = lax.ppermute(right_env, ("sector", "term"), pair_exchange(sectors, 0, 0))
        own_a = lax.ppermute(right_env, ("sector", "term"), pair_exchange(sectors, 1, 1))
        info_own, note, left_own, left_sent, rights = pack(
            kept_rows, op_index, left_env, right_env, half
        )
        left_other = lax.ppermute(left_sent, "term", swap)
        info_other = lax.ppermute(info_own, "term", swap)
        rights += [lax.ppermute(x, "term", swap) for x in rights]
        note = lax.ppermute(note, ("sector", "term"), cycle)
    else:
        forward = [(i, i + 1) for i in range(sectors - 1)]
        backward = [(b, a) for a, b in forward]
        gathered = [lax.all_gather(x, "term", tiled=True) for x in (left_env, right_env, op_index)]
        rows = lax.dynamic_slice_in_dim(gathered[0][:, 0], lax.axis_index("term") * half, half, 1)
        left_own, left_other = jnp.split(rows, 2)
        info_own, info_other = [
            info_of(kept_rows, ops, terms // 2, size) for ops in jnp.split(gathered[2], 2)
        ]
        rights = list(gathered[1][:, 0])

        def neighbour(pairs):
            blocks = lax.all_gather(lax.ppermute(right_env, "sector", pairs), "term", tiled=True)
            return *jnp.split(blocks, 2), lax.ppermute(info_own[0:8, 0:NOTE], "sector", pairs)

        own_a, other_a, note = neighbour(forward)
        own_b, other_b, note_other = neighbour(backward)

    sigma_shape = jax.ShapeDtypeStruct((nvec, 1, 4, half, size), jnp.float32)
    rim_shape = jax.ShapeDtypeStruct((2, terms, nvec * half, size), jnp.bfloat16)
    part_shape = jax.ShapeDtypeStruct((nvec * half, size), jnp.float32)
    params = pltpu.CompilerParams(vmem_limit_bytes=VMEM_LIMIT)

    groups = 2 if nvec % 2 == 0 else 1
    sigma, rim = pl.pallas_call(
        centre_kernel,
        out_shape=(sigma_shape, rim_shape),
        in_specs=[HBM] + [VMEM] * (4 + terms),
        out_specs=(HBM, VMEM),
        scratch_shapes=[
            pltpu.VMEM((nvec, 4, size, size), jnp.bfloat16),
            pltpu.VMEM((terms * half, size), jnp.bfloat16),
            pltpu.VMEM((2, terms, nvec // groups * half, size), jnp.bfloat16),
            pltpu.VMEM((2, nvec, half, size), jnp.float32),
            pltpu.SemaphoreType.DMA((nvec,)),
            pltpu.SemaphoreType.DMA((2, groups)),
        ],
        compiler_params=pltpu.CompilerParams(vmem_limit_bytes=CENTRE_LIMIT),
        name="centre",
    )(psi, info_own, info_other, left_own, left_other, *rights)

    own_a, own_b = own_a.reshape(-1, size), own_b.reshape(-1, size)
    own_b, sigma, rim = lax.optimization_barrier((own_b, sigma, rim))
    own_a, note, sigma = lax.optimization_barrier((own_a, note, sigma))
    if cores == 2:
        other_b = lax.ppermute(own_b, "term", swap)
        other_a = lax.ppermute(own_a, "term", swap)
        note_other = lax.ppermute(note, "term", swap)
    part_a, part_b = pl.pallas_call(
        own_kernel,
        out_shape=(part_shape, part_shape),
        in_specs=[VMEM] * 3,
        out_specs=(VMEM, VMEM),
        compiler_params=params,
        name="own",
    )(rim, own_a, own_b)
    part_b = pl.pallas_call(
        other_kernel,
        out_shape=part_shape,
        in_specs=[VMEM] * 3,
        out_specs=VMEM,
        input_output_aliases={2: 0},
        compiler_params=params,
        name="other",
    )(rim, other_b.reshape(-1, size), part_b)
    return pl.pallas_call(
        last_kernel,
        out_shape=sigma_shape,
        in_specs=[VMEM] * 7 + [HBM],
        out_specs=HBM,
        scratch_shapes=[
            pltpu.VMEM((2, nvec, half, size), jnp.float32),
            pltpu.SemaphoreType.DMA((2, groups)),
        ],
        input_output_aliases={7: 0},
        compiler_params=params,
        name="last",
    )(info_own, note, note_other, rim, other_a.reshape(-1, size), part_a, part_b, sigma)


def solution(mesh):
    in_specs = (
        P(None, "sector", None, None, None),
        P("term", "sector", None, None),
        P("term", "sector", None, None),
        P("term"),
        P("sector"),
    )
    out_specs = P(None, "sector", None, "term", None)
    return jax.shard_map(shards, mesh=mesh, in_specs=in_specs, out_specs=out_specs, check_vma=False)
```

```python
import jax
import jax.numpy as jnp
from jax import lax
from jax.experimental import pallas as pl
from jax.experimental.pallas import tpu as pltpu
from jax.sharding import PartitionSpec as P

FLIP = 2
NOTE = 128
COEFFICIENTS = (
    (1.0, 1.0, 1.0, 1.0),
    (0.25, -0.25, -0.25, 0.25),
    (0.0, 0.5, 0.5, 0.0),
    (0.5, 0.5, -0.5, -0.5),
    (0.5, -0.5, 0.5, -0.5),
)
VMEM_LIMIT = 16 * 1024 * 1024
CENTRE_LIMIT = 50 * 1024 * 1024
PACK_LIMIT = 54579 * 1024
VMEM = pl.BlockSpec(memory_space=pltpu.VMEM)
HBM = pl.BlockSpec(memory_space=pltpu.HBM)


def coefficient(op, p):
    value = jnp.full_like(op, COEFFICIENTS[-1][p])
    for kind in range(len(COEFFICIENTS) - 1):
        value = jnp.where(op == kind, COEFFICIENTS[kind][p], value)
    return value


def times_transpose(a, b):
    return lax.dot_general(a, b, (((1,), (1,)), ((), ())), preferred_element_type=jnp.float32)


def below_is_a():
    return lax.axis_index("sector") % 2 == 0 if lax.axis_size("term") == 2 else True


def info_rows(terms):
    return 16 * pl.cdiv(1 + terms, 16)


def info_of(kept, ops, terms, size, count):
    rows = lax.broadcasted_iota(jnp.int32, (count, size), 0)
    info = jnp.where(rows == 0, kept[0], 0)
    for t in range(terms):
        info = jnp.where(rows == 1 + t, ops[t], info)
    return info.astype(jnp.float32)


def pack_kernel(kept, ops, left, right, info, note, mine, theirs, *refs):
    *blocks, kept_buf, ops_buf, sems = refs
    terms, half, size = mine.shape
    core = lax.axis_index("term")
    scalars = [
        pltpu.make_async_copy(kept, kept_buf, sems.at[0]),
        pltpu.make_async_copy(ops, ops_buf, sems.at[1]),
    ]
    first = [pl.multiple_of(who * half, half) for who in (core, 1 - core)]
    copies = [pltpu.make_async_copy(left.at[:, 0, pl.ds(first[0], half)], mine, sems.at[2])]
    for t, block in enumerate(blocks):
        copies.append(
            pltpu.make_async_copy(
                left.at[t, 0, pl.ds(first[1], half)],
                theirs.at[pl.ds(t * half, half)],
                sems.at[3 + 2 * t],
            )
        )
        copies.append(pltpu.make_async_copy(right.at[t, 0], block, sems.at[4 + 2 * t]))
    for copy in scalars + copies:
        copy.start()
    for copy in scalars:
        copy.wait()
    info[...] = info_of(kept_buf, ops_buf, terms, size, info.shape[0])
    theirs[terms * half:] = info[...].astype(theirs.dtype)
    note[...] = info[0:8, 0:NOTE]
    for copy in copies:
        copy.wait()


def pack(kept, ops, left, right, half):
    terms, size = left.shape[0], left.shape[-1]
    rows = jax.ShapeDtypeStruct((terms, half, size), left.dtype)
    theirs = jax.ShapeDtypeStruct((terms * half + info_rows(terms), size), left.dtype)
    block = jax.ShapeDtypeStruct((size, size), right.dtype)
    info, note, mine, theirs, *blocks = pl.pallas_call(
        pack_kernel,
        out_shape=(jax.ShapeDtypeStruct((info_rows(terms), size), jnp.float32),
                   jax.ShapeDtypeStruct((8, NOTE), jnp.float32), rows, theirs)
        + (block,) * terms,
        in_specs=[HBM] * 4,
        out_specs=(VMEM,) * (4 + terms),
        scratch_shapes=[
            pltpu.SMEM(kept.shape, kept.dtype),
            pltpu.SMEM(ops.shape, ops.dtype),
            pltpu.SemaphoreType.DMA((3 + 2 * terms,)),
        ],
        compiler_params=pltpu.CompilerParams(vmem_limit_bytes=PACK_LIMIT),
        name="pack",
    )(kept, ops, left, right)
    return info, note, mine, theirs, blocks


def centre_kernel(psi, info_own, left_own, left_other, *refs):
    (*rights, sigma, rim, psi_buf, lefts, centre, out_buf, psi_sem, out_sem) = refs
    nvec, half, size = psi.shape[0], sigma.shape[3], psi.shape[4]
    own, terms = left_own.shape[0], len(rights)
    loads = [pltpu.make_async_copy(psi.at[v, 0], psi_buf.at[v], psi_sem.at[v]) for v in range(nvec)]
    for copy in loads:
        copy.start()
    for t in range(own):
        lefts[pl.ds(t * half, half), :] = left_own[t]
    others = (terms - own) * half
    lefts[pl.ds(own * half, others), :] = left_other[:others]
    info_other = left_other[others:].astype(jnp.float32)
    slot_of_3 = jnp.where(below_is_a(), 0, 1)
    ops = [info_own[1 + t:2 + t] if t < own else info_other[1 + t - own:2 + t - own]
           for t in range(terms)]
    factors = [[coefficient(op, p) for p in range(4)] for op in ops]
    flips = [op == FLIP for op in ops]
    rows = lax.broadcasted_iota(jnp.int32, (half, size), 0) + lax.axis_index("term") * half
    cols = lax.broadcasted_iota(jnp.int32, (half, size), 1)
    keep = jnp.maximum(rows, cols).astype(jnp.float32) < info_own[0:1]
    groups = out_sem.shape[1]
    per_group = nvec // groups
    stores = []
    for group in range(groups):
        for j in range(per_group):
            v = group * per_group + j
            loads[v].wait()
            lifted = [
                jnp.dot(lefts[...], psi_buf[v, q], preferred_element_type=jnp.float32)
                for q in range(4)
            ]
            for t in range(terms):
                part = [x[t * half:(t + 1) * half] for x in lifted]
                factor = factors[t]
                for q in (0, 3):
                    slot = slot_of_3 if q == 3 else 1 - slot_of_3
                    rim[slot, t, pl.ds(v * half, half), :] = (part[q] * factor[q]).astype(rim.dtype)
                for p in (1, 2):
                    source = jnp.where(flips[t], part[3 - p], part[p])
                    centre[p - 1, t, pl.ds(j * half, half), :] = (source * factor[p]).astype(
                        centre.dtype
                    )
        for slot in range(2):
            total = None
            for t in range(terms):
                part = times_transpose(centre[slot, t], rights[t][...])
                total = part if total is None else total + part
            for j in range(per_group):
                out_buf[slot, group * per_group + j] = jnp.where(
                    keep, total[j * half:(j + 1) * half], 0.0
                )
            vectors = pl.ds(group * per_group, per_group)
            store = pltpu.make_async_copy(
                out_buf.at[slot, vectors], sigma.at[vectors, 0, slot + 1], out_sem.at[slot, group]
            )
            store.start()
            stores.append(store)
    for store in stores:
        store.wait()


def sum_terms(rim, which, first, blocks, count, rows, total=None):
    size = rim.shape[-1]
    for k in range(count):
        product = times_transpose(rim[which, first + k, rows, :], blocks[k * size:(k + 1) * size])
        total = product if total is None else total + product
    return total


def state_mask(which, info, note, half):
    is_below = (which == 0) == below_is_a()
    me = lax.axis_index("sector")
    there = jnp.where(is_below, me, lax.axis_size("sector") - 1 - me) > 0
    shape = (half, info.shape[1])
    rows = lax.broadcasted_iota(jnp.int32, shape, 0) + lax.axis_index("term") * half
    cols = lax.broadcasted_iota(jnp.int32, shape, 1)
    keep = (rows.astype(jnp.float32) < info[0:1, :]) & there
    return keep & (cols.astype(jnp.float32) < note), jnp.where(is_below, 3, 0)


def crossed():
    return lax.axis_size("term") == 2


def own_kernel(rim, own_a, own_b, part_a, part_b):
    count, rows = own_b.shape[0] // rim.shape[-1], pl.ds(0, rim.shape[2])
    part_a[...] = sum_terms(rim, 0, count if crossed() else 0, own_a, count, rows)
    part_b[...] = sum_terms(rim, 1, 0, own_b, count, rows)


def other_kernel(rim, other_b, part_in, part_b):
    count, rows = other_b.shape[0] // rim.shape[-1], pl.ds(0, rim.shape[2])
    part_b[...] = sum_terms(rim, 1, rim.shape[1] - count, other_b, count, rows, part_in[...])


def last_kernel(info, note, note_other, rim, other_a, part_a, part_b, sigma_in, sigma, out_buf, out_sem):
    _, nvec, half, size = out_buf.shape
    count, groups = other_a.shape[0] // size, out_sem.shape[1]
    first, per_group = 0 if crossed() else rim.shape[1] - count, nvec // groups
    direct = (lax.axis_index("term") == 0) == below_is_a() if lax.axis_size("term") == 2 else True
    notes = [jnp.concatenate([x[0:1, :]] * (size // NOTE), 1) for x in (note, note_other)]
    note_a, note_b = jnp.where(direct, *notes), jnp.where(direct, *notes[::-1])
    stores = []
    for which, note, part in ((1, note_b, part_b), (0, note_a, part_a)):
        keep, state = state_mask(which, info, note, half)
        for group in range(groups):
            rows = pl.ds(group * per_group * half, per_group * half)
            total = part[rows, :]
            if which == 0:
                total = sum_terms(rim, 0, first, other_a, count, rows, total)
            for j in range(per_group):
                out_buf[which, group * per_group + j] = jnp.where(
                    keep, total[j * half:(j + 1) * half], 0.0
                )
            vectors = pl.ds(group * per_group, per_group)
            store = pltpu.make_async_copy(
                out_buf.at[which, vectors], sigma.at[vectors, 0, state], out_sem.at[which, group]
            )
            store.start()
            stores.append(store)
    for store in stores:
        store.wait()


def two_core_cycle(sectors):
    up = [(2 * i, 2 * i + 2) for i in range(sectors - 1)]
    down = [(2 * i + 3, 2 * i + 1) for i in range(sectors - 1)]
    return up + [(2 * sectors - 2, 2 * sectors - 1)] + down + [(1, 0)]


def pair_exchange(sectors, first, cross):
    pairs = []
    for sector in range(sectors):
        low = sector if (sector - first) % 2 == 0 else sector - 1
        alone = low < 0 or low + 1 >= sectors
        for core in range(2):
            target = 2 * sector + 1 - core if alone else 2 * (2 * low + 1 - sector) + (core ^ cross)
            pairs.append((2 * sector + core, target))
    return pairs


def shards(psi, left_env, right_env, op_index, kept_rows):
    sectors, cores = lax.axis_size("sector"), lax.axis_size("term")
    nvec, size = psi.shape[0], psi.shape[-1]
    half = size // cores
    terms = left_env.shape[0] * cores
    swap = [(0, 1), (1, 0)]

    if cores == 2:
        cycle = two_core_cycle(sectors)
        own_b = lax.ppermute(right_env, ("sector", "term"), pair_exchange(sectors, 0, 0))
        own_a = lax.ppermute(right_env, ("sector", "term"), pair_exchange(sectors, 1, 1))
        info_own, note, left_own, left_sent, rights = pack(
            kept_rows, op_index, left_env, right_env, half
        )
        left_other = lax.ppermute(left_sent, "term", swap)
        rights += [lax.ppermute(x, "term", swap) for x in rights]
        note = lax.ppermute(note, ("sector", "term"), cycle)
    else:
        forward = [(i, i + 1) for i in range(sectors - 1)]
        backward = [(b, a) for a, b in forward]
        gathered = [lax.all_gather(x, "term", tiled=True) for x in (left_env, right_env, op_index)]
        rows = lax.dynamic_slice_in_dim(gathered[0][:, 0], lax.axis_index("term") * half, half, 1)
        left_own, left_other = jnp.split(rows, 2)
        info_own, info_other = [
            info_of(kept_rows, ops, terms // 2, size, info_rows(terms // 2))
            for ops in jnp.split(gathered[2], 2)
        ]
        left_other = jnp.concatenate(
            [left_other.reshape(-1, size), info_other.astype(left_other.dtype)], 0
        )
        rights = list(gathered[1][:, 0])

        def neighbour(pairs):
            blocks = lax.all_gather(lax.ppermute(right_env, "sector", pairs), "term", tiled=True)
            return *jnp.split(blocks, 2), lax.ppermute(info_own[0:8, 0:NOTE], "sector", pairs)

        own_a, other_a, note = neighbour(forward)
        own_b, other_b, note_other = neighbour(backward)

    sigma_shape = jax.ShapeDtypeStruct((nvec, 1, 4, half, size), jnp.float32)
    rim_shape = jax.ShapeDtypeStruct((2, terms, nvec * half, size), jnp.bfloat16)
    part_shape = jax.ShapeDtypeStruct((nvec * half, size), jnp.float32)
    params = pltpu.CompilerParams(vmem_limit_bytes=VMEM_LIMIT)

    groups = 2 if nvec % 2 == 0 else 1
    sigma, rim = pl.pallas_call(
        centre_kernel,
        out_shape=(sigma_shape, rim_shape),
        in_specs=[HBM] + [VMEM] * (3 + terms),
        out_specs=(HBM, VMEM),
        scratch_shapes=[
            pltpu.VMEM((nvec, 4, size, size), jnp.bfloat16),
            pltpu.VMEM((terms * half, size), jnp.bfloat16),
            pltpu.VMEM((2, terms, nvec // groups * half, size), jnp.bfloat16),
            pltpu.VMEM((2, nvec, half, size), jnp.float32),
            pltpu.SemaphoreType.DMA((nvec,)),
            pltpu.SemaphoreType.DMA((2, groups)),
        ],
        compiler_params=pltpu.CompilerParams(vmem_limit_bytes=CENTRE_LIMIT),
        name="centre",
    )(psi, info_own, left_own, left_other, *rights)

    own_a, own_b = own_a.reshape(-1, size), own_b.reshape(-1, size)
    own_b, sigma, rim = lax.optimization_barrier((own_b, sigma, rim))
    own_a, note, sigma = lax.optimization_barrier((own_a, note, sigma))
    if cores == 2:
        other_b = lax.ppermute(own_b, "term", swap)
        other_a = lax.ppermute(own_a, "term", swap)
        note_other = lax.ppermute(note, "term", swap)
    part_a, part_b = pl.pallas_call(
        own_kernel,
        out_shape=(part_shape, part_shape),
        in_specs=[VMEM] * 3,
        out_specs=(VMEM, VMEM),
        compiler_params=params,
        name="own",
    )(rim, own_a, own_b)
    part_b = pl.pallas_call(
        other_kernel,
        out_shape=part_shape,
        in_specs=[VMEM] * 3,
        out_specs=VMEM,
        input_output_aliases={2: 0},
        compiler_params=params,
        name="other",
    )(rim, other_b.reshape(-1, size), part_b)
    return pl.pallas_call(
        last_kernel,
        out_shape=sigma_shape,
        in_specs=[VMEM] * 7 + [HBM],
        out_specs=HBM,
        scratch_shapes=[
            pltpu.VMEM((2, nvec, half, size), jnp.float32),
            pltpu.SemaphoreType.DMA((2, 1)),
        ],
        input_output_aliases={7: 0},
        compiler_params=params,
        name="last",
    )(info_own, note, note_other, rim, other_a.reshape(-1, size), part_a, part_b, sigma)


def solution(mesh):
    in_specs = (
        P(None, "sector", None, None, None),
        P("term", "sector", None, None),
        P("term", "sector", None, None),
        P("term"),
        P("sector"),
    )
    out_specs = P(None, "sector", None, "term", None)
    return jax.shard_map(shards, mesh=mesh, in_specs=in_specs, out_specs=out_specs, check_vma=False)
```

```python
import jax
import jax.numpy as jnp
from jax import lax
from jax.experimental import pallas as pl
from jax.experimental.pallas import tpu as pltpu
from jax.sharding import PartitionSpec as P

FLIP = 2
NOTE = 128
COEFFICIENTS = (
    (1.0, 1.0, 1.0, 1.0),
    (0.25, -0.25, -0.25, 0.25),
    (0.0, 0.5, 0.5, 0.0),
    (0.5, 0.5, -0.5, -0.5),
    (0.5, -0.5, 0.5, -0.5),
)
VMEM_LIMIT = 16 * 1024 * 1024
CENTRE_LIMIT = 50 * 1024 * 1024
PACK_LIMIT = 54579 * 1024
VMEM = pl.BlockSpec(memory_space=pltpu.VMEM)
HBM = pl.BlockSpec(memory_space=pltpu.HBM)


def coefficient(op, p):
    value = jnp.full_like(op, COEFFICIENTS[-1][p])
    for kind in range(len(COEFFICIENTS) - 1):
        value = jnp.where(op == kind, COEFFICIENTS[kind][p], value)
    return value


def times_transpose(a, b):
    return lax.dot_general(a, b, (((1,), (1,)), ((), ())), preferred_element_type=jnp.float32)


def below_is_a():
    return lax.axis_index("sector") % 2 == 0 if lax.axis_size("term") == 2 else True


def info_rows(terms):
    return 16 * pl.cdiv(1 + terms, 16)


def info_of(kept, ops, terms, size, count):
    rows = lax.broadcasted_iota(jnp.int32, (count, size), 0)
    info = jnp.where(rows == 0, kept[0], 0)
    for t in range(terms):
        info = jnp.where(rows == 1 + t, ops[t], info)
    return info.astype(jnp.float32)


def pack_kernel(kept, ops, left, right, info, note, mine, theirs, *refs):
    *blocks, kept_buf, ops_buf, sems = refs
    terms, half, size = mine.shape
    core = lax.axis_index("term")
    scalars = [
        pltpu.make_async_copy(kept, kept_buf, sems.at[0]),
        pltpu.make_async_copy(ops, ops_buf, sems.at[1]),
    ]
    first = [pl.multiple_of(who * half, half) for who in (core, 1 - core)]
    copies = [pltpu.make_async_copy(left.at[:, 0, pl.ds(first[0], half)], mine, sems.at[2])]
    for t, block in enumerate(blocks):
        copies.append(
            pltpu.make_async_copy(
                left.at[t, 0, pl.ds(first[1], half)],
                theirs.at[pl.ds(t * half, half)],
                sems.at[3 + 2 * t],
            )
        )
        copies.append(pltpu.make_async_copy(right.at[t, 0], block, sems.at[4 + 2 * t]))
    for copy in scalars + copies:
        copy.start()
    for copy in scalars:
        copy.wait()
    info[...] = info_of(kept_buf, ops_buf, terms, size, info.shape[0])
    theirs[terms * half:] = info[...].astype(theirs.dtype)
    note[...] = info[0:8, 0:NOTE]
    for copy in copies:
        copy.wait()


def pack(kept, ops, left, right, half):
    terms, size = left.shape[0], left.shape[-1]
    rows = jax.ShapeDtypeStruct((terms, half, size), left.dtype)
    theirs = jax.ShapeDtypeStruct((terms * half + info_rows(terms), size), left.dtype)
    block = jax.ShapeDtypeStruct((size, size), right.dtype)
    info, note, mine, theirs, *blocks = pl.pallas_call(
        pack_kernel,
        out_shape=(jax.ShapeDtypeStruct((info_rows(terms), size), jnp.float32),
                   jax.ShapeDtypeStruct((8, NOTE), jnp.float32), rows, theirs)
        + (block,) * terms,
        in_specs=[HBM] * 4,
        out_specs=(VMEM,) * (4 + terms),
        scratch_shapes=[
            pltpu.SMEM(kept.shape, kept.dtype),
            pltpu.SMEM(ops.shape, ops.dtype),
            pltpu.SemaphoreType.DMA((3 + 2 * terms,)),
        ],
        compiler_params=pltpu.CompilerParams(vmem_limit_bytes=PACK_LIMIT),
        name="pack",
    )(kept, ops, left, right)
    return info, note, mine, theirs, blocks


def centre_kernel(psi, info_own, left_own, left_other, *refs):
    (*rights, sigma, rim, psi_buf, lefts, centre, out_buf, psi_sem, out_sem) = refs
    nvec, half, size = psi.shape[0], sigma.shape[3], psi.shape[4]
    own, terms = left_own.shape[0], len(rights)
    loads = [pltpu.make_async_copy(psi.at[v, 0], psi_buf.at[v], psi_sem.at[v]) for v in range(nvec)]
    for copy in loads:
        copy.start()
    for t in range(own):
        lefts[pl.ds(t * half, half), :] = left_own[t]
    others = (terms - own) * half
    lefts[pl.ds(own * half, others), :] = left_other[:others]
    info_other = left_other[others:].astype(jnp.float32)
    slot_of_3 = jnp.where(below_is_a(), 0, 1)
    ops = [info_own[1 + t:2 + t] if t < own else info_other[1 + t - own:2 + t - own]
           for t in range(terms)]
    factors = [[coefficient(op, p) for p in range(4)] for op in ops]
    flips = [op == FLIP for op in ops]
    rows = lax.broadcasted_iota(jnp.int32, (half, size), 0) + lax.axis_index("term") * half
    cols = lax.broadcasted_iota(jnp.int32, (half, size), 1)
    keep = jnp.maximum(rows, cols).astype(jnp.float32) < info_own[0:1]
    groups = out_sem.shape[1]
    per_group = nvec // groups
    stores = []
    for group in range(groups):
        for j in range(per_group):
            v = group * per_group + j
            loads[v].wait()
            lifted = [
                jnp.dot(lefts[...], psi_buf[v, q], preferred_element_type=jnp.float32)
                for q in range(4)
            ]
            for t in range(terms):
                part = [x[t * half:(t + 1) * half] for x in lifted]
                factor = factors[t]
                for q in (0, 3):
                    slot = slot_of_3 if q == 3 else 1 - slot_of_3
                    rim[slot, t, pl.ds(v * half, half), :] = (part[q] * factor[q]).astype(rim.dtype)
                for p in (1, 2):
                    source = jnp.where(flips[t], part[3 - p], part[p])
                    centre[p - 1, t, pl.ds(j * half, half), :] = (source * factor[p]).astype(
                        centre.dtype
                    )
        for slot in range(2):
            total = None
            for t in range(terms):
                part = times_transpose(centre[slot, t], rights[t][...])
                total = part if total is None else total + part
            for j in range(per_group):
                out_buf[slot, group * per_group + j] = jnp.where(
                    keep, total[j * half:(j + 1) * half], 0.0
                )
            vectors = pl.ds(group * per_group, per_group)
            store = pltpu.make_async_copy(
                out_buf.at[slot, vectors], sigma.at[vectors, 0, slot + 1], out_sem.at[slot, group]
            )
            store.start()
            stores.append(store)
    for store in stores:
        store.wait()


def sum_terms(rim, which, first, blocks, count, rows, total=None):
    size = rim.shape[-1]
    for k in range(count):
        product = times_transpose(rim[which, first + k, rows, :], blocks[k * size:(k + 1) * size])
        total = product if total is None else total + product
    return total


def state_mask(which, info, note, half):
    is_below = (which == 0) == below_is_a()
    me = lax.axis_index("sector")
    there = jnp.where(is_below, me, lax.axis_size("sector") - 1 - me) > 0
    shape = (half, info.shape[1])
    rows = lax.broadcasted_iota(jnp.int32, shape, 0) + lax.axis_index("term") * half
    cols = lax.broadcasted_iota(jnp.int32, shape, 1)
    keep = (rows.astype(jnp.float32) < info[0:1, :]) & there
    return keep & (cols.astype(jnp.float32) < note), jnp.where(is_below, 3, 0)


def crossed():
    return lax.axis_size("term") == 2


def own_kernel(rim, own_a, own_b, part_a, part_b):
    count, rows = own_b.shape[0] // rim.shape[-1], pl.ds(0, rim.shape[2])
    part_a[...] = sum_terms(rim, 0, count if crossed() else 0, own_a, count, rows)
    part_b[...] = sum_terms(rim, 1, 0, own_b, count, rows)


def other_kernel(rim, other_b, part_in, part_b):
    count, rows = other_b.shape[0] // rim.shape[-1], pl.ds(0, rim.shape[2])
    part_b[...] = sum_terms(rim, 1, rim.shape[1] - count, other_b, count, rows, part_in[...])


def last_kernel(info, note, note_other, rim, other_a, part_a, part_b, sigma_in, sigma, out_buf, out_sem):
    _, nvec, half, size = out_buf.shape
    count, groups = other_a.shape[0] // size, out_sem.shape[1]
    first, per_group = 0 if crossed() else rim.shape[1] - count, nvec // groups
    direct = (lax.axis_index("term") == 0) == below_is_a() if lax.axis_size("term") == 2 else True
    notes = [jnp.concatenate([x[0:1, :]] * (size // NOTE), 1) for x in (note, note_other)]
    note_a, note_b = jnp.where(direct, *notes), jnp.where(direct, *notes[::-1])
    stores = []
    for which, note, part in ((1, note_b, part_b), (0, note_a, part_a)):
        keep, state = state_mask(which, info, note, half)
        for group in range(groups):
            rows = pl.ds(group * per_group * half, per_group * half)
            total = part[rows, :]
            if which == 0:
                total = sum_terms(rim, 0, first, other_a, count, rows, total)
            for j in range(per_group):
                out_buf[which, group * per_group + j] = jnp.where(
                    keep, total[j * half:(j + 1) * half], 0.0
                )
            vectors = pl.ds(group * per_group, per_group)
            store = pltpu.make_async_copy(
                out_buf.at[which, vectors], sigma.at[vectors, 0, state], out_sem.at[which, group]
            )
            store.start()
            stores.append(store)
    for store in stores:
        store.wait()


def two_core_cycle(sectors):
    up = [(2 * i, 2 * i + 2) for i in range(sectors - 1)]
    down = [(2 * i + 3, 2 * i + 1) for i in range(sectors - 1)]
    return up + [(2 * sectors - 2, 2 * sectors - 1)] + down + [(1, 0)]


def pair_exchange(sectors, first, cross):
    pairs = []
    for sector in range(sectors):
        low = sector if (sector - first) % 2 == 0 else sector - 1
        alone = low < 0 or low + 1 >= sectors
        for core in range(2):
            target = 2 * sector + 1 - core if alone else 2 * (2 * low + 1 - sector) + (core ^ cross)
            pairs.append((2 * sector + core, target))
    return pairs


def shards(psi, left_env, right_env, op_index, kept_rows):
    sectors, cores = lax.axis_size("sector"), lax.axis_size("term")
    nvec, size = psi.shape[0], psi.shape[-1]
    half = size // cores
    terms = left_env.shape[0] * cores
    swap = [(0, 1), (1, 0)]

    if cores == 2:
        cycle = two_core_cycle(sectors)
        own_b = lax.ppermute(right_env, ("sector", "term"), pair_exchange(sectors, 0, 0))
        own_a = lax.ppermute(right_env, ("sector", "term"), pair_exchange(sectors, 1, 1))
        info_own, note, left_own, left_sent, rights = pack(
            kept_rows, op_index, left_env, right_env, half
        )
        left_other = lax.ppermute(left_sent, "term", swap)
        rights += [lax.ppermute(x, "term", swap) for x in rights]
        note = lax.ppermute(note, ("sector", "term"), cycle)
    else:
        forward = [(i, i + 1) for i in range(sectors - 1)]
        backward = [(b, a) for a, b in forward]
        gathered = [lax.all_gather(x, "term", tiled=True) for x in (left_env, right_env, op_index)]
        rows = lax.dynamic_slice_in_dim(gathered[0][:, 0], lax.axis_index("term") * half, half, 1)
        left_own, left_other = jnp.split(rows, 2)
        info_own, info_other = [
            info_of(kept_rows, ops, terms // 2, size, info_rows(terms // 2))
            for ops in jnp.split(gathered[2], 2)
        ]
        left_other = jnp.concatenate(
            [left_other.reshape(-1, size), info_other.astype(left_other.dtype)], 0
        )
        rights = list(gathered[1][:, 0])

        def neighbour(pairs):
            blocks = lax.all_gather(lax.ppermute(right_env, "sector", pairs), "term", tiled=True)
            return *jnp.split(blocks, 2), lax.ppermute(info_own[0:8, 0:NOTE], "sector", pairs)

        own_a, other_a, note = neighbour(forward)
        own_b, other_b, note_other = neighbour(backward)

    sigma_shape = jax.ShapeDtypeStruct((nvec, 1, 4, half, size), jnp.float32)
    rim_shape = jax.ShapeDtypeStruct((2, terms, nvec * half, size), jnp.bfloat16)
    part_shape = jax.ShapeDtypeStruct((nvec * half, size), jnp.float32)
    params = pltpu.CompilerParams(vmem_limit_bytes=VMEM_LIMIT)

    groups = 2 if nvec % 2 == 0 else 1
    sigma, rim = pl.pallas_call(
        centre_kernel,
        out_shape=(sigma_shape, rim_shape),
        in_specs=[HBM] + [VMEM] * (3 + terms),
        out_specs=(HBM, VMEM),
        scratch_shapes=[
            pltpu.VMEM((nvec, 4, size, size), jnp.bfloat16),
            pltpu.VMEM((terms * half, size), jnp.bfloat16),
            pltpu.VMEM((2, terms, nvec // groups * half, size), jnp.bfloat16),
            pltpu.VMEM((2, nvec, half, size), jnp.float32),
            pltpu.SemaphoreType.DMA((nvec,)),
            pltpu.SemaphoreType.DMA((2, groups)),
        ],
        compiler_params=pltpu.CompilerParams(vmem_limit_bytes=CENTRE_LIMIT),
        name="centre",
    )(psi, info_own, left_own, left_other, *rights)

    own_a, own_b = own_a.reshape(-1, size), own_b.reshape(-1, size)
    own_b, sigma, rim = lax.optimization_barrier((own_b, sigma, rim))
    note, sigma = lax.optimization_barrier((note, sigma))
    own_a, sigma = lax.optimization_barrier((own_a, sigma))
    if cores == 2:
        other_b = lax.ppermute(own_b, "term", swap)
        other_a = lax.ppermute(own_a, "term", swap)
        note_other = lax.ppermute(note, "term", swap)
    part_a, part_b = pl.pallas_call(
        own_kernel,
        out_shape=(part_shape, part_shape),
        in_specs=[VMEM] * 3,
        out_specs=(VMEM, VMEM),
        compiler_params=params,
        name="own",
    )(rim, own_a, own_b)
    part_b = pl.pallas_call(
        other_kernel,
        out_shape=part_shape,
        in_specs=[VMEM] * 3,
        out_specs=VMEM,
        input_output_aliases={2: 0},
        compiler_params=params,
        name="other",
    )(rim, other_b.reshape(-1, size), part_b)
    return pl.pallas_call(
        last_kernel,
        out_shape=sigma_shape,
        in_specs=[VMEM] * 7 + [HBM],
        out_specs=HBM,
        scratch_shapes=[
            pltpu.VMEM((2, nvec, half, size), jnp.float32),
            pltpu.SemaphoreType.DMA((2, 1)),
        ],
        input_output_aliases={7: 0},
        compiler_params=params,
        name="last",
    )(info_own, note, note_other, rim, other_a.reshape(-1, size), part_a, part_b, sigma)


def solution(mesh):
    in_specs = (
        P(None, "sector", None, None, None),
        P("term", "sector", None, None),
        P("term", "sector", None, None),
        P("term"),
        P("sector"),
    )
    out_specs = P(None, "sector", None, "term", None)
    return jax.shard_map(shards, mesh=mesh, in_specs=in_specs, out_specs=out_specs, check_vma=False)
```

```python
import jax
import jax.numpy as jnp
from jax import lax
from jax.experimental import pallas as pl
from jax.experimental.pallas import tpu as pltpu
from jax.sharding import PartitionSpec as P

FLIP = 2
NOTE = 128
COEFFICIENTS = (
    (1.0, 1.0, 1.0, 1.0),
    (0.25, -0.25, -0.25, 0.25),
    (0.0, 0.5, 0.5, 0.0),
    (0.5, 0.5, -0.5, -0.5),
    (0.5, -0.5, 0.5, -0.5),
)
VMEM_LIMIT = 16 * 1024 * 1024
CENTRE_LIMIT = 50 * 1024 * 1024
PACK_LIMIT = 54579 * 1024
VMEM = pl.BlockSpec(memory_space=pltpu.VMEM)
HBM = pl.BlockSpec(memory_space=pltpu.HBM)


def coefficient(op, p):
    value = jnp.full_like(op, COEFFICIENTS[-1][p])
    for kind in range(len(COEFFICIENTS) - 1):
        value = jnp.where(op == kind, COEFFICIENTS[kind][p], value)
    return value


def times_transpose(a, b):
    return lax.dot_general(a, b, (((1,), (1,)), ((), ())), preferred_element_type=jnp.float32)


def below_is_a():
    return lax.axis_index("sector") % 2 == 0 if lax.axis_size("term") == 2 else True


def info_rows(terms):
    return 16 * pl.cdiv(1 + terms, 16)


def info_of(kept, ops, terms, size, count):
    rows = lax.broadcasted_iota(jnp.int32, (count, size), 0)
    info = jnp.where(rows == 0, kept[0], 0)
    for t in range(terms):
        info = jnp.where(rows == 1 + t, ops[t], info)
    return info.astype(jnp.float32)


def pack_kernel(kept, ops, left, right, info, note, mine, theirs, *refs):
    *blocks, kept_buf, ops_buf, sems = refs
    terms, half, size = mine.shape
    core = lax.axis_index("term")
    scalars = [
        pltpu.make_async_copy(kept, kept_buf, sems.at[0]),
        pltpu.make_async_copy(ops, ops_buf, sems.at[1]),
    ]
    first = [pl.multiple_of(who * half, half) for who in (core, 1 - core)]
    copies = [pltpu.make_async_copy(left.at[:, 0, pl.ds(first[0], half)], mine, sems.at[2])]
    for t, block in enumerate(blocks):
        copies.append(
            pltpu.make_async_copy(
                left.at[t, 0, pl.ds(first[1], half)],
                theirs.at[pl.ds(t * half, half)],
                sems.at[3 + 2 * t],
            )
        )
        copies.append(pltpu.make_async_copy(right.at[t, 0], block, sems.at[4 + 2 * t]))
    for copy in scalars + copies:
        copy.start()
    for copy in scalars:
        copy.wait()
    info[...] = info_of(kept_buf, ops_buf, terms, size, info.shape[0])
    theirs[terms * half:] = info[...].astype(theirs.dtype)
    note[...] = info[0:8, 0:NOTE]
    for copy in copies:
        copy.wait()


def pack(kept, ops, left, right, half):
    terms, size = left.shape[0], left.shape[-1]
    rows = jax.ShapeDtypeStruct((terms, half, size), left.dtype)
    theirs = jax.ShapeDtypeStruct((terms * half + info_rows(terms), size), left.dtype)
    block = jax.ShapeDtypeStruct((size, size), right.dtype)
    info, note, mine, theirs, *blocks = pl.pallas_call(
        pack_kernel,
        out_shape=(jax.ShapeDtypeStruct((info_rows(terms), size), jnp.float32),
                   jax.ShapeDtypeStruct((8, NOTE), jnp.float32), rows, theirs)
        + (block,) * terms,
        in_specs=[HBM] * 4,
        out_specs=(VMEM,) * (4 + terms),
        scratch_shapes=[
            pltpu.SMEM(kept.shape, kept.dtype),
            pltpu.SMEM(ops.shape, ops.dtype),
            pltpu.SemaphoreType.DMA((3 + 2 * terms,)),
        ],
        compiler_params=pltpu.CompilerParams(vmem_limit_bytes=PACK_LIMIT),
        name="pack",
    )(kept, ops, left, right)
    return info, note, mine, theirs, blocks


def centre_kernel(psi, info_own, left_own, left_other, *refs):
    (*rights, sigma, rim, psi_buf, lefts, centre, out_buf, psi_sem, out_sem) = refs
    nvec, half, size = psi.shape[0], sigma.shape[3], psi.shape[4]
    own, terms = left_own.shape[0], len(rights)
    loads = [pltpu.make_async_copy(psi.at[v, 0], psi_buf.at[v], psi_sem.at[v]) for v in range(nvec)]
    for copy in loads:
        copy.start()
    for t in range(own):
        lefts[pl.ds(t * half, half), :] = left_own[t]
    others = (terms - own) * half
    lefts[pl.ds(own * half, others), :] = left_other[:others]
    info_other = left_other[others:].astype(jnp.float32)
    slot_of_3 = jnp.where(below_is_a(), 0, 1)
    ops = [info_own[1 + t:2 + t] if t < own else info_other[1 + t - own:2 + t - own]
           for t in range(terms)]
    factors = [[coefficient(op, p) for p in range(4)] for op in ops]
    flips = [op == FLIP for op in ops]
    rows = lax.broadcasted_iota(jnp.int32, (half, size), 0) + lax.axis_index("term") * half
    cols = lax.broadcasted_iota(jnp.int32, (half, size), 1)
    keep = jnp.maximum(rows, cols).astype(jnp.float32) < info_own[0:1]
    groups = out_sem.shape[1]
    per_group = nvec // groups
    stores = []
    for group in range(groups):
        for j in range(per_group):
            v = group * per_group + j
            loads[v].wait()
            lifted = [
                jnp.dot(lefts[...], psi_buf[v, q], preferred_element_type=jnp.float32)
                for q in range(4)
            ]
            for t in range(terms):
                part = [x[t * half:(t + 1) * half] for x in lifted]
                factor = factors[t]
                for q in (0, 3):
                    slot = slot_of_3 if q == 3 else 1 - slot_of_3
                    rim[slot, t, pl.ds(v * half, half), :] = (part[q] * factor[q]).astype(rim.dtype)
                for p in (1, 2):
                    source = jnp.where(flips[t], part[3 - p], part[p])
                    centre[p - 1, t, pl.ds(j * half, half), :] = (source * factor[p]).astype(
                        centre.dtype
                    )
        for slot in range(2):
            total = None
            for t in range(terms):
                part = times_transpose(centre[slot, t], rights[t][...])
                total = part if total is None else total + part
            for j in range(per_group):
                out_buf[slot, group * per_group + j] = jnp.where(
                    keep, total[j * half:(j + 1) * half], 0.0
                )
            vectors = pl.ds(group * per_group, per_group)
            store = pltpu.make_async_copy(
                out_buf.at[slot, vectors], sigma.at[vectors, 0, slot + 1], out_sem.at[slot, group]
            )
            store.start()
            stores.append(store)
    for store in stores:
        store.wait()


def sum_terms(rim, which, first, blocks, count, rows, total=None):
    size = rim.shape[-1]
    for k in range(count):
        product = times_transpose(rim[which, first + k, rows, :], blocks[k * size:(k + 1) * size])
        total = product if total is None else total + product
    return total


def state_mask(which, info, note, half):
    is_below = (which == 0) == below_is_a()
    me = lax.axis_index("sector")
    there = jnp.where(is_below, me, lax.axis_size("sector") - 1 - me) > 0
    shape = (half, info.shape[1])
    rows = lax.broadcasted_iota(jnp.int32, shape, 0) + lax.axis_index("term") * half
    cols = lax.broadcasted_iota(jnp.int32, shape, 1)
    keep = (rows.astype(jnp.float32) < info[0:1, :]) & there
    return keep & (cols.astype(jnp.float32) < note), jnp.where(is_below, 3, 0)


def crossed():
    return lax.axis_size("term") == 2


def own_kernel(rim, own_a, own_b, part_a, part_b):
    count, rows = own_b.shape[0] // rim.shape[-1], pl.ds(0, rim.shape[2])
    part_a[...] = sum_terms(rim, 0, count if crossed() else 0, own_a, count, rows)
    part_b[...] = sum_terms(rim, 1, 0, own_b, count, rows)


def other_kernel(rim, other_b, part_c):
    count, rows = other_b.shape[0] // rim.shape[-1], pl.ds(0, rim.shape[2])
    part_c[...] = sum_terms(rim, 1, rim.shape[1] - count, other_b, count, rows)


def last_kernel(info, note, note_other, rim, other_a, part_a, part_b, part_c, sigma_in, sigma, out_buf,
                out_sem):
    _, nvec, half, size = out_buf.shape
    count, groups = other_a.shape[0] // size, out_sem.shape[1]
    first, per_group = 0 if crossed() else rim.shape[1] - count, nvec // groups
    direct = (lax.axis_index("term") == 0) == below_is_a() if lax.axis_size("term") == 2 else True
    notes = [jnp.concatenate([x[0:1, :]] * (size // NOTE), 1) for x in (note, note_other)]
    note_a, note_b = jnp.where(direct, *notes), jnp.where(direct, *notes[::-1])
    stores = []
    for which, note, part in ((1, note_b, part_b), (0, note_a, part_a)):
        keep, state = state_mask(which, info, note, half)
        for group in range(groups):
            rows = pl.ds(group * per_group * half, per_group * half)
            total = part[rows, :]
            if which == 0:
                total = sum_terms(rim, 0, first, other_a, count, rows, total)
            else:
                total = total + part_c[rows, :]
            for j in range(per_group):
                out_buf[which, group * per_group + j] = jnp.where(
                    keep, total[j * half:(j + 1) * half], 0.0
                )
            vectors = pl.ds(group * per_group, per_group)
            store = pltpu.make_async_copy(
                out_buf.at[which, vectors], sigma.at[vectors, 0, state], out_sem.at[which, group]
            )
            store.start()
            stores.append(store)
    for store in stores:
        store.wait()


def two_core_cycle(sectors):
    up = [(2 * i, 2 * i + 2) for i in range(sectors - 1)]
    down = [(2 * i + 3, 2 * i + 1) for i in range(sectors - 1)]
    return up + [(2 * sectors - 2, 2 * sectors - 1)] + down + [(1, 0)]


def pair_exchange(sectors, first, cross):
    pairs = []
    for sector in range(sectors):
        low = sector if (sector - first) % 2 == 0 else sector - 1
        alone = low < 0 or low + 1 >= sectors
        for core in range(2):
            target = 2 * sector + 1 - core if alone else 2 * (2 * low + 1 - sector) + (core ^ cross)
            pairs.append((2 * sector + core, target))
    return pairs


def shards(psi, left_env, right_env, op_index, kept_rows):
    sectors, cores = lax.axis_size("sector"), lax.axis_size("term")
    nvec, size = psi.shape[0], psi.shape[-1]
    half = size // cores
    terms = left_env.shape[0] * cores
    swap = [(0, 1), (1, 0)]

    if cores == 2:
        cycle = two_core_cycle(sectors)
        own_b = lax.ppermute(right_env, ("sector", "term"), pair_exchange(sectors, 0, 0))
        own_a = lax.ppermute(right_env, ("sector", "term"), pair_exchange(sectors, 1, 1))
        info_own, note, left_own, left_sent, rights = pack(
            kept_rows, op_index, left_env, right_env, half
        )
        left_other = lax.ppermute(left_sent, "term", swap)
        rights += [lax.ppermute(x, "term", swap) for x in rights]
        note = lax.ppermute(note, ("sector", "term"), cycle)
    else:
        forward = [(i, i + 1) for i in range(sectors - 1)]
        backward = [(b, a) for a, b in forward]
        gathered = [lax.all_gather(x, "term", tiled=True) for x in (left_env, right_env, op_index)]
        rows = lax.dynamic_slice_in_dim(gathered[0][:, 0], lax.axis_index("term") * half, half, 1)
        left_own, left_other = jnp.split(rows, 2)
        info_own, info_other = [
            info_of(kept_rows, ops, terms // 2, size, info_rows(terms // 2))
            for ops in jnp.split(gathered[2], 2)
        ]
        left_other = jnp.concatenate(
            [left_other.reshape(-1, size), info_other.astype(left_other.dtype)], 0
        )
        rights = list(gathered[1][:, 0])

        def neighbour(pairs):
            blocks = lax.all_gather(lax.ppermute(right_env, "sector", pairs), "term", tiled=True)
            return *jnp.split(blocks, 2), lax.ppermute(info_own[0:8, 0:NOTE], "sector", pairs)

        own_a, other_a, note = neighbour(forward)
        own_b, other_b, note_other = neighbour(backward)

    sigma_shape = jax.ShapeDtypeStruct((nvec, 1, 4, half, size), jnp.float32)
    rim_shape = jax.ShapeDtypeStruct((2, terms, nvec * half, size), jnp.bfloat16)
    part_shape = jax.ShapeDtypeStruct((nvec * half, size), jnp.float32)
    params = pltpu.CompilerParams(vmem_limit_bytes=VMEM_LIMIT)

    groups = 2 if nvec % 2 == 0 else 1
    sigma, rim = pl.pallas_call(
        centre_kernel,
        out_shape=(sigma_shape, rim_shape),
        in_specs=[HBM] + [VMEM] * (3 + terms),
        out_specs=(HBM, VMEM),
        scratch_shapes=[
            pltpu.VMEM((nvec, 4, size, size), jnp.bfloat16),
            pltpu.VMEM((terms * half, size), jnp.bfloat16),
            pltpu.VMEM((2, terms, nvec // groups * half, size), jnp.bfloat16),
            pltpu.VMEM((2, nvec, half, size), jnp.float32),
            pltpu.SemaphoreType.DMA((nvec,)),
            pltpu.SemaphoreType.DMA((2, groups)),
        ],
        compiler_params=pltpu.CompilerParams(vmem_limit_bytes=CENTRE_LIMIT),
        name="centre",
    )(psi, info_own, left_own, left_other, *rights)

    own_a, own_b = own_a.reshape(-1, size), own_b.reshape(-1, size)
    own_b, sigma, rim = lax.optimization_barrier((own_b, sigma, rim))
    own_a, note, sigma = lax.optimization_barrier((own_a, note, sigma))
    if cores == 2:
        other_b = lax.ppermute(own_b, "term", swap)
        other_a = lax.ppermute(own_a, "term", swap)
        note_other = lax.ppermute(note, "term", swap)
    part_a, part_b = pl.pallas_call(
        own_kernel,
        out_shape=(part_shape, part_shape),
        in_specs=[VMEM] * 3,
        out_specs=(VMEM, VMEM),
        compiler_params=params,
        name="own",
    )(rim, own_a, own_b)
    part_c = pl.pallas_call(
        other_kernel,
        out_shape=part_shape,
        in_specs=[VMEM] * 2,
        out_specs=VMEM,
        compiler_params=params,
        name="other",
    )(rim, other_b.reshape(-1, size))
    return pl.pallas_call(
        last_kernel,
        out_shape=sigma_shape,
        in_specs=[VMEM] * 8 + [HBM],
        out_specs=HBM,
        scratch_shapes=[
            pltpu.VMEM((2, nvec, half, size), jnp.float32),
            pltpu.SemaphoreType.DMA((2, 1)),
        ],
        input_output_aliases={8: 0},
        compiler_params=params,
        name="last",
    )(info_own, note, note_other, rim, other_a.reshape(-1, size), part_a, part_b, part_c, sigma)


def solution(mesh):
    in_specs = (
        P(None, "sector", None, None, None),
        P("term", "sector", None, None),
        P("term", "sector", None, None),
        P("term"),
        P("sector"),
    )
    out_specs = P(None, "sector", None, "term", None)
    return jax.shard_map(shards, mesh=mesh, in_specs=in_specs, out_specs=out_specs, check_vma=False)
```

```python
import jax
import jax.numpy as jnp
from jax import lax
from jax.experimental import pallas as pl
from jax.experimental.pallas import tpu as pltpu
from jax.sharding import PartitionSpec as P

FLIP = 2
NOTE = 128
COEFFICIENTS = (
    (1.0, 1.0, 1.0, 1.0),
    (0.25, -0.25, -0.25, 0.25),
    (0.0, 0.5, 0.5, 0.0),
    (0.5, 0.5, -0.5, -0.5),
    (0.5, -0.5, 0.5, -0.5),
)
VMEM_LIMIT = 16 * 1024 * 1024
CENTRE_LIMIT = 50 * 1024 * 1024
PACK_LIMIT = 54579 * 1024
VMEM = pl.BlockSpec(memory_space=pltpu.VMEM)
HBM = pl.BlockSpec(memory_space=pltpu.HBM)


def coefficient(op, p):
    value = jnp.full_like(op, COEFFICIENTS[-1][p])
    for kind in range(len(COEFFICIENTS) - 1):
        value = jnp.where(op == kind, COEFFICIENTS[kind][p], value)
    return value


def times_transpose(a, b):
    return lax.dot_general(a, b, (((1,), (1,)), ((), ())), preferred_element_type=jnp.float32)


def below_is_a():
    return lax.axis_index("sector") % 2 == 0 if lax.axis_size("term") == 2 else True


def info_rows(terms):
    return 16 * pl.cdiv(1 + terms, 16)


def info_of(kept, ops, terms, size, count):
    rows = lax.broadcasted_iota(jnp.int32, (count, size), 0)
    info = jnp.where(rows == 0, kept[0], 0)
    for t in range(terms):
        info = jnp.where(rows == 1 + t, ops[t], info)
    return info.astype(jnp.float32)


def pack_kernel(kept, ops, left, right, info, note, mine, theirs, *refs):
    *blocks, kept_buf, ops_buf, sems = refs
    terms, half, size = mine.shape
    core = lax.axis_index("term")
    scalars = [
        pltpu.make_async_copy(kept, kept_buf, sems.at[0]),
        pltpu.make_async_copy(ops, ops_buf, sems.at[1]),
    ]
    first = [pl.multiple_of(who * half, half) for who in (core, 1 - core)]
    copies = [pltpu.make_async_copy(left.at[:, 0, pl.ds(first[0], half)], mine, sems.at[2])]
    for t, block in enumerate(blocks):
        copies.append(
            pltpu.make_async_copy(
                left.at[t, 0, pl.ds(first[1], half)],
                theirs.at[pl.ds(t * half, half)],
                sems.at[3 + 2 * t],
            )
        )
        copies.append(pltpu.make_async_copy(right.at[t, 0], block, sems.at[4 + 2 * t]))
    for copy in scalars + copies:
        copy.start()
    for copy in scalars:
        copy.wait()
    info[...] = info_of(kept_buf, ops_buf, terms, size, info.shape[0])
    theirs[terms * half:] = info[...].astype(theirs.dtype)
    note[...] = info[0:8, 0:NOTE]
    for copy in copies:
        copy.wait()


def pack(kept, ops, left, right, half):
    terms, size = left.shape[0], left.shape[-1]
    rows = jax.ShapeDtypeStruct((terms, half, size), left.dtype)
    theirs = jax.ShapeDtypeStruct((terms * half + info_rows(terms), size), left.dtype)
    block = jax.ShapeDtypeStruct((size, size), right.dtype)
    info, note, mine, theirs, *blocks = pl.pallas_call(
        pack_kernel,
        out_shape=(jax.ShapeDtypeStruct((info_rows(terms), size), jnp.float32),
                   jax.ShapeDtypeStruct((8, NOTE), jnp.float32), rows, theirs)
        + (block,) * terms,
        in_specs=[HBM] * 4,
        out_specs=(VMEM,) * (4 + terms),
        scratch_shapes=[
            pltpu.SMEM(kept.shape, kept.dtype),
            pltpu.SMEM(ops.shape, ops.dtype),
            pltpu.SemaphoreType.DMA((3 + 2 * terms,)),
        ],
        compiler_params=pltpu.CompilerParams(vmem_limit_bytes=PACK_LIMIT),
        name="pack",
    )(kept, ops, left, right)
    return info, note, mine, theirs, blocks


def centre_kernel(psi, info_own, left_own, left_other, *refs):
    (*rights, sigma, rim, psi_buf, lefts, centre, out_buf, psi_sem, out_sem) = refs
    nvec, half, size = psi.shape[0], sigma.shape[3], psi.shape[4]
    own, terms = left_own.shape[0], len(rights)
    loads = [pltpu.make_async_copy(psi.at[v, 0], psi_buf.at[v], psi_sem.at[v]) for v in range(nvec)]
    for copy in loads:
        copy.start()
    for t in range(own):
        lefts[pl.ds(t * half, half), :] = left_own[t]
    others = (terms - own) * half
    lefts[pl.ds(own * half, others), :] = left_other[:others]
    info_other = left_other[others:].astype(jnp.float32)
    slot_of_3 = jnp.where(below_is_a(), 0, 1)
    ops = [info_own[1 + t:2 + t] if t < own else info_other[1 + t - own:2 + t - own]
           for t in range(terms)]
    factors = [[coefficient(op, p) for p in range(4)] for op in ops]
    flips = [op == FLIP for op in ops]
    rows = lax.broadcasted_iota(jnp.int32, (half, size), 0) + lax.axis_index("term") * half
    cols = lax.broadcasted_iota(jnp.int32, (half, size), 1)
    keep = jnp.maximum(rows, cols).astype(jnp.float32) < info_own[0:1]
    groups = out_sem.shape[1]
    per_group = nvec // groups
    stores = []
    for group in range(groups):
        for j in range(per_group):
            v = group * per_group + j
            loads[v].wait()
            lifted = [
                jnp.dot(lefts[...], psi_buf[v, q], preferred_element_type=jnp.float32)
                for q in range(4)
            ]
            for t in range(terms):
                part = [x[t * half:(t + 1) * half] for x in lifted]
                factor = factors[t]
                for q in (0, 3):
                    slot = slot_of_3 if q == 3 else 1 - slot_of_3
                    rim[slot, t, pl.ds(v * half, half), :] = (part[q] * factor[q]).astype(rim.dtype)
                for p in (1, 2):
                    source = jnp.where(flips[t], part[3 - p], part[p])
                    centre[p - 1, t, pl.ds(j * half, half), :] = (source * factor[p]).astype(
                        centre.dtype
                    )
        for slot in range(2):
            total = None
            for t in range(terms):
                part = times_transpose(centre[slot, t], rights[t][...])
                total = part if total is None else total + part
            for j in range(per_group):
                out_buf[slot, group * per_group + j] = jnp.where(
                    keep, total[j * half:(j + 1) * half], 0.0
                )
            vectors = pl.ds(group * per_group, per_group)
            store = pltpu.make_async_copy(
                out_buf.at[slot, vectors], sigma.at[vectors, 0, slot + 1], out_sem.at[slot, group]
            )
            store.start()
            stores.append(store)
    for store in stores:
        store.wait()


def sum_terms(rim, which, first, blocks, count, rows, total=None):
    size = rim.shape[-1]
    for k in range(count):
        product = times_transpose(rim[which, first + k, rows, :], blocks[k * size:(k + 1) * size])
        total = product if total is None else total + product
    return total


def state_mask(which, info, note, half):
    is_below = (which == 0) == below_is_a()
    me = lax.axis_index("sector")
    there = jnp.where(is_below, me, lax.axis_size("sector") - 1 - me) > 0
    shape = (half, info.shape[1])
    rows = lax.broadcasted_iota(jnp.int32, shape, 0) + lax.axis_index("term") * half
    cols = lax.broadcasted_iota(jnp.int32, shape, 1)
    keep = (rows.astype(jnp.float32) < info[0:1, :]) & there
    return keep & (cols.astype(jnp.float32) < note), jnp.where(is_below, 3, 0)


def crossed():
    return lax.axis_size("term") == 2


def own_kernel(rim, own_a, own_b, part_a, part_b):
    count, rows = own_b.shape[0] // rim.shape[-1], pl.ds(0, rim.shape[2])
    part_a[...] = sum_terms(rim, 0, count if crossed() else 0, own_a, count, rows)
    part_b[...] = sum_terms(rim, 1, 0, own_b, count, rows)


def other_kernel(rim, other_b, part_in, part_b):
    count, rows = other_b.shape[0] // rim.shape[-1], pl.ds(0, rim.shape[2])
    part_b[...] = sum_terms(rim, 1, rim.shape[1] - count, other_b, count, rows, part_in[...])


def last_kernel(info, note, note_other, rim, other_a, part_a, part_b, sigma_in, sigma, out_buf, out_sem):
    _, nvec, half, size = out_buf.shape
    count = other_a.shape[0] // size
    first = 0 if crossed() else rim.shape[1] - count
    direct = (lax.axis_index("term") == 0) == below_is_a() if lax.axis_size("term") == 2 else True
    notes = [jnp.concatenate([x[0:1, :]] * (size // NOTE), 1) for x in (note, note_other)]
    note_a, note_b = jnp.where(direct, *notes), jnp.where(direct, *notes[::-1])
    stores = []
    for which, note, part in ((1, note_b, part_b), (0, note_a, part_a)):
        keep, state = state_mask(which, info, note, half)
        groups = out_sem.shape[1] if which == 0 else 1
        per_group = nvec // groups
        for group in range(groups):
            rows = pl.ds(group * per_group * half, per_group * half)
            total = part[rows, :]
            if which == 0:
                total = sum_terms(rim, 0, first, other_a, count, rows, total)
            for j in range(per_group):
                out_buf[which, group * per_group + j] = jnp.where(
                    keep, total[j * half:(j + 1) * half], 0.0
                )
            vectors = pl.ds(group * per_group, per_group)
            store = pltpu.make_async_copy(
                out_buf.at[which, vectors], sigma.at[vectors, 0, state], out_sem.at[which, group]
            )
            store.start()
            stores.append(store)
    for store in stores:
        store.wait()


def two_core_cycle(sectors):
    up = [(2 * i, 2 * i + 2) for i in range(sectors - 1)]
    down = [(2 * i + 3, 2 * i + 1) for i in range(sectors - 1)]
    return up + [(2 * sectors - 2, 2 * sectors - 1)] + down + [(1, 0)]


def pair_exchange(sectors, first, cross):
    pairs = []
    for sector in range(sectors):
        low = sector if (sector - first) % 2 == 0 else sector - 1
        alone = low < 0 or low + 1 >= sectors
        for core in range(2):
            target = 2 * sector + 1 - core if alone else 2 * (2 * low + 1 - sector) + (core ^ cross)
            pairs.append((2 * sector + core, target))
    return pairs


def shards(psi, left_env, right_env, op_index, kept_rows):
    sectors, cores = lax.axis_size("sector"), lax.axis_size("term")
    nvec, size = psi.shape[0], psi.shape[-1]
    half = size // cores
    terms = left_env.shape[0] * cores
    swap = [(0, 1), (1, 0)]

    if cores == 2:
        cycle = two_core_cycle(sectors)
        own_b = lax.ppermute(right_env, ("sector", "term"), pair_exchange(sectors, 0, 0))
        own_a = lax.ppermute(right_env, ("sector", "term"), pair_exchange(sectors, 1, 1))
        info_own, note, left_own, left_sent, rights = pack(
            kept_rows, op_index, left_env, right_env, half
        )
        left_other = lax.ppermute(left_sent, "term", swap)
        rights += [lax.ppermute(x, "term", swap) for x in rights]
        note = lax.ppermute(note, ("sector", "term"), cycle)
    else:
        forward = [(i, i + 1) for i in range(sectors - 1)]
        backward = [(b, a) for a, b in forward]
        gathered = [lax.all_gather(x, "term", tiled=True) for x in (left_env, right_env, op_index)]
        rows = lax.dynamic_slice_in_dim(gathered[0][:, 0], lax.axis_index("term") * half, half, 1)
        left_own, left_other = jnp.split(rows, 2)
        info_own, info_other = [
            info_of(kept_rows, ops, terms // 2, size, info_rows(terms // 2))
            for ops in jnp.split(gathered[2], 2)
        ]
        left_other = jnp.concatenate(
            [left_other.reshape(-1, size), info_other.astype(left_other.dtype)], 0
        )
        rights = list(gathered[1][:, 0])

        def neighbour(pairs):
            blocks = lax.all_gather(lax.ppermute(right_env, "sector", pairs), "term", tiled=True)
            return *jnp.split(blocks, 2), lax.ppermute(info_own[0:8, 0:NOTE], "sector", pairs)

        own_a, other_a, note = neighbour(forward)
        own_b, other_b, note_other = neighbour(backward)

    sigma_shape = jax.ShapeDtypeStruct((nvec, 1, 4, half, size), jnp.float32)
    rim_shape = jax.ShapeDtypeStruct((2, terms, nvec * half, size), jnp.bfloat16)
    part_shape = jax.ShapeDtypeStruct((nvec * half, size), jnp.float32)
    params = pltpu.CompilerParams(vmem_limit_bytes=VMEM_LIMIT)

    groups = 2 if nvec % 2 == 0 else 1
    sigma, rim = pl.pallas_call(
        centre_kernel,
        out_shape=(sigma_shape, rim_shape),
        in_specs=[HBM] + [VMEM] * (3 + terms),
        out_specs=(HBM, VMEM),
        scratch_shapes=[
            pltpu.VMEM((nvec, 4, size, size), jnp.bfloat16),
            pltpu.VMEM((terms * half, size), jnp.bfloat16),
            pltpu.VMEM((2, terms, nvec // groups * half, size), jnp.bfloat16),
            pltpu.VMEM((2, nvec, half, size), jnp.float32),
            pltpu.SemaphoreType.DMA((nvec,)),
            pltpu.SemaphoreType.DMA((2, groups)),
        ],
        compiler_params=pltpu.CompilerParams(vmem_limit_bytes=CENTRE_LIMIT),
        name="centre",
    )(psi, info_own, left_own, left_other, *rights)

    own_a, own_b = own_a.reshape(-1, size), own_b.reshape(-1, size)
    own_b, sigma, rim = lax.optimization_barrier((own_b, sigma, rim))
    own_a, note, sigma = lax.optimization_barrier((own_a, note, sigma))
    if cores == 2:
        other_b = lax.ppermute(own_b, "term", swap)
        other_a = lax.ppermute(own_a, "term", swap)
        note_other = lax.ppermute(note, "term", swap)
    part_a, part_b = pl.pallas_call(
        own_kernel,
        out_shape=(part_shape, part_shape),
        in_specs=[VMEM] * 3,
        out_specs=(VMEM, VMEM),
        compiler_params=params,
        name="own",
    )(rim, own_a, own_b)
    part_b = pl.pallas_call(
        other_kernel,
        out_shape=part_shape,
        in_specs=[VMEM] * 3,
        out_specs=VMEM,
        input_output_aliases={2: 0},
        compiler_params=params,
        name="other",
    )(rim, other_b.reshape(-1, size), part_b)
    return pl.pallas_call(
        last_kernel,
        out_shape=sigma_shape,
        in_specs=[VMEM] * 7 + [HBM],
        out_specs=HBM,
        scratch_shapes=[
            pltpu.VMEM((2, nvec, half, size), jnp.float32),
            pltpu.SemaphoreType.DMA((2, groups)),
        ],
        input_output_aliases={7: 0},
        compiler_params=params,
        name="last",
    )(info_own, note, note_other, rim, other_a.reshape(-1, size), part_a, part_b, sigma)


def solution(mesh):
    in_specs = (
        P(None, "sector", None, None, None),
        P("term", "sector", None, None),
        P("term", "sector", None, None),
        P("term"),
        P("sector"),
    )
    out_specs = P(None, "sector", None, "term", None)
    return jax.shard_map(shards, mesh=mesh, in_specs=in_specs, out_specs=out_specs, check_vma=False)
```
